128 devices in a mesh: comp: 2 (over core), tile: 64 (over x, y, z).
Axes of the slice: x: 4, y: 4, z: 4, core: 2. Of those that a mesh axis runs over, the one named last changes fastest.
Arguments:
- state_field: float32 [2, 8, 24, 16, 8192], P('comp', None, None, None, 'tile'), may hold values from -6 to 6
- courant: float32 [2, 2, 8, 16, 8192], P('comp', None, None, None, 'tile'), may hold values from -0.3 to 0.3
- diffusivity: float32 [2, 8, 16, 8192], P('comp', None, None, 'tile'), may hold values from 0.1 to 10
- coupling_rate: float32 [2, 16, 8192], P('comp', None, 'tile'), may hold values from 0.2 to 1
- weight_table: bfloat16 [32, 128, 128], replicated, may hold values from -0.5 to 0.5
- source_row: int32 [2, 64, 384], P('comp', 'tile'), may hold values from 0 to 15
- destination_tile_ids: int32 [2, 64, 384, 1], P('comp', 'tile'), may hold values from 0 to 63; in each aligned block of 384 rows (0 to 383, 384 to 767, ..., all dimensions but the last counted through in order) at most 8 rows name the same one
- dest_row: int32 [2, 64, 384], P('comp', 'tile'), may hold values from 0 to 15
- weight_slot: int32 [2, 64, 384], P('comp', 'tile'), may hold values from 0 to 31
Outputs:
- new_state: float32 [2, 8, 24, 16, 8192], P('comp', None, None, None, 'tile')
The draws below stay inside these ranges and needn't reach their ends.
Inputs may be any that keep to these rules, and one draw needn't show every extreme that they name: `destination_tile_ids`: among the 384 entries of one device no destination tile is named more than 8 times, and that bound is reached.
All inputs are finite; a program needn't handle non-finite values.
Results may differ from the reference program's by a relative error of at most 0.0037.
Values may be sent and summed in bfloat16 or wider, within the bound.
A program may use at most 128 MiB of HBM per device.

```python
import math
import jax
import jax.numpy as jnp
import numpy as np
from jax import lax

LEV = 8
FIELDS = 24
CY = 16
CX = 128
STEPS = 4
CAP = 8
ENTRIES = 384
WTAB = 32
TILES = 64
NX = 8192
N_TILE = 64


def with_ends(result, own_key, low, largest):
    longest = result.shape.index(max(result.shape))
    spots = []
    for shift in (0, 1):
        where = [jax.random.randint(jax.random.fold_in(own_key, axis), (), 0, length) for axis, length in enumerate(result.shape)]
        where[longest] = (where[longest] + shift) % result.shape[longest]
        spots.append(tuple(where))
    return result.at[spots[0]].set(low).at[spots[1]].set(largest)


def block_levels(own_key, extent, split, low, high):
    def one(dim, blocks):
        steps = jax.random.uniform(jax.random.fold_in(jax.random.fold_in(own_key, 6), dim), (blocks,), jnp.float32, low / len(split), high / len(split))
        return jnp.repeat(jnp.exp(steps), extent[dim] // blocks).reshape((-1,) + (1,) * (len(extent) - dim - 1))

    factor_of = one(*split[0])
    for cut in split[1:]:
        factor_of = factor_of * one(*cut)
    return factor_of


def shared_out(key, own, number, rows, amount, top, reach, lean):
    ranking = jax.random.permutation(key, amount)
    packed, usual = shares(amount, rows * top, reach, lean, True), shares(amount, rows * top, reach, lean, False)
    places = jnp.arange(amount)

    def named(tallies, turn):
        used = int((tallies > 0).sum())
        fixed = max(1, used // 4)
        shifted = fixed + (places - fixed + turn * (used - fixed)) % max(1, amount - fixed)
        return jnp.zeros((amount,), jnp.int32).at[ranking[jnp.where(places < fixed, places, shifted)]].set(jnp.asarray(tallies, jnp.int32))

    tallies = jnp.where(number % 4 == 0, named(packed, number // 4), named(usual, number - number // 4 - 1))
    mixed = jax.random.permutation(jax.random.fold_in(own, 3), amount)
    donor, receiver = mixed[0:amount // 2 * 2:2], mixed[1:amount // 2 * 2:2]
    slack = jnp.minimum(tallies[donor] - 1, reach - tallies[receiver]) // 2
    slack = jnp.where((donor == ranking[0]) | (receiver == ranking[0]) | (tallies[receiver] == 0), 0, jnp.maximum(slack, 0))
    shifted = jax.random.randint(jax.random.fold_in(own, 4), (amount // 2,), 0, 1 << 20) % (slack + 1)
    tallies = tallies.at[donor].add(-shifted).at[receiver].add(shifted)
    labels = jnp.searchsorted(jnp.cumsum(tallies), jnp.arange(rows * top), side="right").astype(jnp.int32)
    grid = labels.reshape(top, rows).T
    grid = grid[jax.random.permutation(jax.random.fold_in(own, 1), rows)]
    turn = jax.random.randint(jax.random.fold_in(own, 2), (rows, 1), 0, top)
    return jnp.take_along_axis(grid, (jnp.arange(top)[None, :] + turn) % top, axis=1)


def shares(amount, total, bound, lean, full):
    loads = [(1 << 20) // math.isqrt(rank ** lean) + 1 for rank in range(1, amount + 1)]
    largest = bound if full else min(bound, max(-(-total // amount), total * loads[0] // sum(loads)))
    least = 1 if total - largest >= amount - 1 else 0
    holding, spare = [largest] + [least] * (amount - 1), total - largest - least * (amount - 1)
    while spare > 0:
        candidates = [i for i in range(1, amount) if holding[i] < largest] or [i for i in range(1, amount) if holding[i] < bound]
        whole, remaining = sum([loads[i] for i in candidates]), spare
        for i in candidates:
            more = min(bound - holding[i], max(1, remaining * loads[i] // whole), spare)
            holding[i] = holding[i] + more
            spare = spare - more
    return np.array(holding)


def gaussian(rng, dims, scale, bound, split=(), held_as=jnp.bfloat16):
    loudness = block_levels(rng, dims, split, -0.22, 0.18) if split else 1.0
    drawn = jax.random.normal(rng, dims, jnp.float32) * scale * loudness
    return jnp.minimum(jnp.maximum(drawn, -bound), bound).astype(held_as)


def setup_inputs(seed: int = 0) -> dict:
    key_list = jax.random.split(jax.random.key(seed), 10)
    state_field = gaussian(key_list[0], (2, LEV, FIELDS, CY, NX), 1.0, 6.0, ((0, 2), (4, 64)), jnp.float32)
    courant = jnp.clip(jax.random.uniform(key_list[1], (2, 2, LEV, CY, NX), jnp.float32, -0.3, 0.3) * block_levels(key_list[1], (2, 2, LEV, CY, NX), ((0, 2), (4, 64)), -0.4, 0.0), -0.3, 0.3)
    diffusivity = jnp.clip(jnp.exp(math.log(10.0) - 4.6051702 * jax.random.uniform(key_list[2], (2, LEV, CY, NX), jnp.float32) ** block_levels(key_list[2], (2, LEV, CY, NX), ((0, 2), (3, 64)), -0.2, 0.2)), 0.1, 10.0)
    coupling_rate = jnp.clip(0.2 + 0.8 * jax.random.uniform(key_list[3], (2, CY, NX), jnp.float32) ** block_levels(key_list[3], (2, CY, NX), ((0, 2), (2, 64)), -0.2, 0.2), 0.2, 1.0)
    weight_table = gaussian(key_list[4], (WTAB, CX, CX), CX ** -0.5, 0.5)
    source_row = with_ends(jax.random.randint(key_list[5], (2, TILES, ENTRIES), 0, CY), jax.random.fold_in(key_list[5], 1), 0, CY - 1).astype(jnp.int32)
    destination_tile_ids_keys = jax.random.split(jax.random.fold_in(key_list[6], 1), 2 * TILES * ENTRIES // ENTRIES)
    destination_tile_ids_turns = jax.random.permutation(jax.random.fold_in(key_list[6], 3), 2 * TILES * ENTRIES // ENTRIES)
    destination_tile_ids = jax.vmap(lambda own, number: shared_out(jax.random.fold_in(key_list[6], 2), own, number, ENTRIES, N_TILE, 1, CAP, 2))(destination_tile_ids_keys, destination_tile_ids_turns).reshape((2, TILES, ENTRIES, 1))
    dest_row = with_ends(jax.random.randint(key_list[7], (2, TILES, ENTRIES), 0, CY), jax.random.fold_in(key_list[7], 1), 0, CY - 1).astype(jnp.int32)
    weight_slot = with_ends(jax.random.randint(key_list[8], (2, TILES, ENTRIES), 0, WTAB), jax.random.fold_in(key_list[8], 1), 0, WTAB - 1).astype(jnp.int32)
    return {"state_field": state_field, "courant": courant, "diffusivity": diffusivity, "coupling_rate": coupling_rate, "weight_table": weight_table, "source_row": source_row, "destination_tile_ids": destination_tile_ids, "dest_row": dest_row, "weight_slot": weight_slot}


def transport(tracer, courant_x, courant_y):
    flux_x = jnp.maximum(courant_x, 0.0)[:, :, None] * tracer + jnp.minimum(courant_x, 0.0)[:, :, None] * jnp.roll(tracer, -1, axis=-1)
    inner_y = courant_y[:, :, :-1, :]
    flux_inner = jnp.maximum(inner_y, 0.0)[:, :, None] * tracer[..., :-1, :] + jnp.minimum(inner_y, 0.0)[:, :, None] * tracer[..., 1:, :]
    zero_row = jnp.zeros_like(tracer[..., :1, :])
    flux_high = jnp.concatenate([flux_inner, zero_row], axis=-2)
    flux_low = jnp.concatenate([zero_row, flux_inner], axis=-2)
    return tracer - (flux_x - jnp.roll(flux_x, 1, axis=-1)) - (flux_high - flux_low)


def vertical_solve(rhs, diffusivity):
    levels = diffusivity.shape[1]
    level_ids = jnp.arange(levels).reshape(1, levels, 1, 1)
    above = jnp.where(level_ids < levels - 1, diffusivity, jnp.zeros_like(diffusivity))
    below = jnp.concatenate([jnp.zeros_like(above[:, :1]), above[:, :-1]], axis=1)

    def forward(carry, level):
        ratio_prev, solved_prev = carry
        below_k, above_k, rhs_k = level
        pivot = 1.0 + below_k + above_k - below_k * ratio_prev
        ratio = above_k / pivot
        solved = (rhs_k + below_k[:, None] * solved_prev) / pivot[:, None]
        return (ratio, solved), (ratio, solved)

    start = (jnp.zeros_like(above[:, 0]), jnp.zeros_like(rhs[:, 0]))
    moved = (jnp.moveaxis(below, 1, 0), jnp.moveaxis(above, 1, 0), jnp.moveaxis(rhs, 1, 0))
    unused, (ratios, solveds) = lax.scan(forward, start, moved)

    def backward(upper, level):
        ratio, solved = level
        value = solved + ratio[:, None] * upper
        return value, value

    unused_top, values = lax.scan(backward, jnp.zeros_like(rhs[:, 0]), (ratios, solveds), reverse=True)
    return jnp.moveaxis(values, 0, 1)


def reference(state_field, courant, diffusivity, coupling_rate, weight_table, source_row, destination_tile_ids, dest_row, weight_slot):
    tiles = N_TILE
    surface = state_field[:, 0].astype(jnp.bfloat16)
    by_source = surface.reshape(2, FIELDS, CY, tiles, CX).transpose(0, 3, 2, 1, 4).reshape(2 * tiles, CY, FIELDS, CX)
    rows_picked = source_row.reshape(2 * tiles, ENTRIES).astype(jnp.int32)
    slots_picked = weight_slot.reshape(2 * tiles, ENTRIES).astype(jnp.int32)

    def contribute(item):
        blocks, picks, weight_picks = item
        chosen = blocks[picks].astype(jnp.float32)
        matrices = weight_table[weight_picks].astype(jnp.float32)
        return jnp.einsum("efb,ecb->efc", chosen, matrices, precision=lax.Precision.HIGHEST).astype(jnp.bfloat16)

    contribution = lax.map(contribute, (by_source, rows_picked, slots_picked))
    comp_of = (jnp.arange(2 * tiles) // tiles).astype(jnp.int32)
    target = ((1 - comp_of)[:, None] * tiles + destination_tile_ids.reshape(2 * tiles, ENTRIES).astype(jnp.int32)) * CY + dest_row.reshape(2 * tiles, ENTRIES).astype(jnp.int32)
    incoming = jnp.zeros((2 * tiles * CY, FIELDS, CX), jnp.float32)
    incoming = incoming.at[target.reshape(-1)].add(contribution.reshape(-1, FIELDS, CX).astype(jnp.float32))
    incoming = incoming.reshape(2, tiles, CY, FIELDS, CX).transpose(0, 3, 2, 1, 4).reshape(2, FIELDS, CY, tiles * CX)
    advected = state_field
    for substep in range(STEPS):
        advected = transport(advected, courant[:, 0], courant[:, 1])
    rhs = advected.at[:, 0].add(coupling_rate[:, None] * incoming)
    return vertical_solve(rhs, diffusivity)
```

```python
import functools

import jax
import jax.numpy as jnp
from jax import lax
from jax.experimental import pallas as pl
from jax.experimental.pallas import tpu as pltpu
from jax.sharding import PartitionSpec as P

MESH = pl.DeviceIdType.MESH
NT = (((1,), (1,)), ((), ()))
STEPS = 4
LEV, FIELDS, CY, CX = 8, 24, 16, 128
ENTRIES, WTAB = 384, 32
GROUPS = 3
GF = FIELDS // GROUPS
SLABS = GF + 1
STRIDE = (16, 4, 1)
AXES = ((0, 1, 2), (1, 2, 0), (2, 0, 1))
F32, BF16, I32 = jnp.float32, jnp.bfloat16, jnp.int32


def iota(shape, dim):
    return lax.broadcasted_iota(I32, shape, dim)


def roll_lanes(value, shift):
    return pltpu.roll(value, shift % CX, 1)


def stencil_coefs(cx, cy):
    rows = iota(cx.shape, 0)
    cxp, cxm = jnp.maximum(cx, 0.0), jnp.minimum(cx, 0.0)
    cy = jnp.where(rows < CY - 1, cy, 0.0)
    cyp, cym = jnp.maximum(cy, 0.0), jnp.minimum(cy, 0.0)
    west = roll_lanes(cxp, 1)
    south = pltpu.roll(cyp, 1, 0)
    centre = 1.0 - cxp + roll_lanes(cxm, 1) - cyp + pltpu.roll(cym, 1, 0)
    return centre, -cxm, west, -cym, south


def advance(a, coefs):
    centre, east, west, north, south = coefs
    for step in range(STEPS):
        a = (
            centre * a
            + east * roll_lanes(a, CX - 1)
            + west * roll_lanes(a, 1)
            + north * pltpu.roll(a, CY - 1, 0)
            + south * pltpu.roll(a, 1, 0)
        )
    return a


def replicate(value):
    for shift in (16, 32, 64):
        value = value + roll_lanes(value, shift)
    return value


def kernel(
    state_hbm,
    courant_ref,
    diff_ref,
    rate_ref,
    weight_hbm,
    srow_ref,
    dest_ref,
    drow_ref,
    wslot_ref,
    solved_hbm,
    gain_ref,
    incoming_ref,
    state,
    weight,
    packed,
    cpacked,
    halo_out,
    halo_in,
    fixed,
    gath,
    pick,
    spread,
    outgoing,
    arrived,
    solve_coef,
    load_sem,
    weight_sem,
    store_sem,
    ag_send,
    ag_recv,
    halo_send,
    halo_recv,
    sc_send,
    sc_recv,
):
    comp, tile = lax.axis_index("comp"), lax.axis_index("tile")
    coords = (tile >> 4, (tile >> 2) & 3, tile & 3)

    def shifted(axis, step):
        return tile + (((coords[axis] + step) & 3) - coords[axis]) * STRIDE[axis]

    loads = [
        pltpu.make_async_copy(state_hbm.at[k], state.at[k], load_sem.at[k]) for k in range(LEV)
    ]
    for load in loads:
        load.start()
    weight_load = pltpu.make_async_copy(weight_hbm, weight, weight_sem)
    weight_load.start()

    right, left = (tile + 1) & 63, (tile + 63) & 63
    barrier = pltpu.get_barrier_semaphore()
    greeted = [(comp, shifted(axis, step)) for axis in range(3) for step in (1, 3)]
    greeted += [(comp, right), (comp, left), (1 - comp, tile)]
    greeted += [(1 - comp, shifted(axis, step)) for axis in range(3) for step in (1, 2, 3)]
    for target in greeted:
        pl.semaphore_signal(barrier, inc=1, device_id=target, device_id_type=MESH)

    targets = dest_ref[...]
    srow, drow, wslot = srow_ref[...], drow_ref[...], wslot_ref[...]
    named = (iota((64, ENTRIES), 0) == targets).astype(F32)
    before = (iota((ENTRIES, ENTRIES), 0) < iota((ENTRIES, ENTRIES), 1)).astype(F32)
    counts = jnp.dot(named.astype(BF16), before.astype(BF16), preferred_element_type=F32)
    rank = jnp.sum(named * counts, axis=0, keepdims=True).astype(I32)
    rel = (
        ((targets >> 4) - coords[0]) & 3,
        ((targets >> 2) - coords[1]) & 3,
        (targets - coords[2]) & 3,
    )
    kind, quarter = iota((16, ENTRIES), 0) >> 2, iota((16, ENTRIES), 0) & 3
    values = jnp.where(kind == 0, wslot, jnp.where(kind == 1, srow, drow + 1))
    for g, (u, v, q) in enumerate(AXES):
        spot = (rel[u] * 4 + rel[v]) * 8 + rank
        hot = (iota((CX, ENTRIES), 0) == spot).astype(F32).astype(BF16)
        kept = jnp.where((quarter == rel[q]) & (kind < 3), values, 0)
        table = lax.dot_general(kept.astype(F32).astype(BF16), hot, NT, preferred_element_type=F32)
        gath[g, 0, 0, GF] = table.astype(BF16)

    loads[0].wait()
    for g in range(GROUPS):
        gath[g, 0, 0, :GF] = state[0, g * GF : (g + 1) * GF].astype(BF16)

    pl.semaphore_wait(barrier, len(greeted))

    def remote(src, dst, send, recv, target):
        return pltpu.make_async_remote_copy(
            src_ref=src,
            dst_ref=dst,
            send_sem=send,
            recv_sem=recv,
            device_id=target,
            device_id_type=MESH,
        )

    def gather_copy(g, number):
        u, v, q = AXES[g]
        half = 5
        src, dst, axis, step = (
            (gath.at[g, 0, 0], gath.at[g, 0, 3], u, 1),
            (gath.at[g, 0, 0], gath.at[g, 0, 1], u, 3),
            (gath.at[g, 0, 3, pl.ds(0, half)], gath.at[g, 0, 2, pl.ds(0, half)], u, 1),
            (gath.at[g, 0, 1, pl.ds(half, SLABS - half)], gath.at[g, 0, 2, pl.ds(half, SLABS - half)], u, 3),
            (gath.at[g, 0], gath.at[g, 3], v, 1),
            (gath.at[g, 0], gath.at[g, 1], v, 3),
            (gath.at[g, 3, pl.ds(0, 2)], gath.at[g, 2, pl.ds(0, 2)], v, 1),
            (gath.at[g, 1, pl.ds(2, 2)], gath.at[g, 2, pl.ds(2, 2)], v, 3),
        )[number]
        return remote(src, dst, ag_send.at[g, number], ag_recv.at[g, number], (comp, shifted(axis, step)))

    gathers = [[gather_copy(g, number) for number in range(8)] for g in range(GROUPS)]

    def start_pair(phase):
        for g in range(GROUPS):
            gathers[g][2 * phase].start()
            gathers[g][2 * phase + 1].start()

    def wait_pair(phase):
        for g in range(GROUPS):
            gathers[g][2 * phase].wait_recv()
            gathers[g][2 * phase + 1].wait_recv()

    start_pair(0)

    for load in loads[1:]:
        load.wait()
    lanes = iota((CY, CX), 1)
    group_of, place = lanes >> 4, lanes & 15

    def pack_level(k, carry):
        for m in range(GROUPS):
            value = roll_lanes(state[k, m * 8], 8)
            for i in range(1, 8):
                value = jnp.where(group_of == i, roll_lanes(state[k, m * 8 + i], 16 * i + 8), value)
            packed[k * 3 + m] = value
        for c in range(2):
            cpacked[c, k] = replicate(jnp.where(lanes < 16, roll_lanes(courant_ref[c, k], 8), 0.0))
        return carry

    lax.fori_loop(0, LEV, pack_level, 0)
    quad = (lanes >> 2) & 3
    for n in range(6):
        for side, base in ((0, 4), (1, 8)):
            value = roll_lanes(packed[4 * n], -base)
            for t in range(1, 4):
                value = jnp.where(quad == t, roll_lanes(packed[4 * n + t], 4 * t - base), value)
            halo_out[side, n] = value
    for side, base in ((0, 4), (1, 8)):
        value = roll_lanes(cpacked[0, 0], -base)
        for e in range(1, 16):
            moved = roll_lanes(cpacked[e // 8, e % 8], 4 * (e % 4) - base)
            value = jnp.where((lanes >> 2) == e, moved, value)
        halo_out[side, 6] = value
    halos = [
        remote(halo_out.at[side], halo_in.at[side], halo_send.at[side], halo_recv.at[side], (comp, target))
        for side, target in ((0, right), (1, left))
    ]
    for copy in halos:
        copy.start()

    wait_pair(0)
    start_pair(1)

    def transport_level(k, carry):
        coefs = stencil_coefs(courant_ref[0, k], courant_ref[1, k])

        def fields(n, inner):
            for j in range(4):
                state[k, n * 4 + j] = advance(state[k, n * 4 + j], coefs)
            return inner

        return lax.fori_loop(0, FIELDS // 4, fields, carry)

    lax.fori_loop(0, 1, transport_level, 0)
    wait_pair(1)
    start_pair(2)
    lax.fori_loop(1, 6, transport_level, 0)
    wait_pair(2)
    start_pair(3)
    lax.fori_loop(6, LEV, transport_level, 0)

    ratio = jnp.zeros((CY, CX), F32)
    gain = None
    gains, ratios = [], []
    for k in range(LEV):
        above = diff_ref[k] if k < LEV - 1 else jnp.zeros((CY, CX), F32)
        below = diff_ref[k - 1] if k > 0 else jnp.zeros((CY, CX), F32)
        inverse = 1.0 / (1.0 + below + above - below * ratio)
        ratio = above * inverse
        solve_coef[0, k] = inverse
        solve_coef[1, k] = below * inverse
        solve_coef[2, k] = ratio
        gain = inverse if k == 0 else below * inverse * gain
        gains.append(gain)
        ratios.append(ratio)
    value = jnp.zeros((CY, CX), F32)
    for k in reversed(range(LEV)):
        value = gains[k] + ratios[k] * value
        gain_ref[k] = value * rate_ref[...]

    for copy in halos:
        copy.wait_recv()

    def strip_level(k, carry):
        cl, cr = [], []
        for c in range(2):
            e = c * 8 + k
            from_left = roll_lanes(halo_in[0, 6], CX - 4 * e)
            from_right = roll_lanes(halo_in[1, 6], CX - 4 * e)
            from_left = replicate(jnp.where(lanes < 4, from_left, 0.0))
            from_right = replicate(jnp.where(lanes < 4, from_right, 0.0))
            own = cpacked[c, k]
            cl.append(jnp.where(place < 4, from_left, roll_lanes(own, -4)))
            cr.append(jnp.where((place >= 8) & (place < 12), roll_lanes(from_right, 8), own))
        coefs_left, coefs_right = stencil_coefs(*cl), stencil_coefs(*cr)
        for m in range(3):
            p = k * 3 + m
            n, t = p >> 2, p & 3
            own = packed[p]
            a_left = jnp.where(place < 4, roll_lanes(halo_in[0, n], CX - 4 * t), roll_lanes(own, -4))
            a_right = jnp.where(
                (place >= 8) & (place < 12), roll_lanes(halo_in[1, n], CX + 8 - 4 * t), own
            )
            a_left, a_right = advance(a_left, coefs_left), advance(a_right, coefs_right)
            fixed[p] = jnp.where(place < 4, roll_lanes(a_right, -4), a_left)
        return carry

    lax.fori_loop(0, LEV, strip_level, 0)

    weight_load.wait()
    rows_p, rows_q = iota((WTAB * CY, CX), 0), iota((256, CX), 0)
    lane_p = iota((1, CX), 1) >> 3
    scatters = []
    for g, (u, v, q) in enumerate(AXES):
        for number in (6, 7):
            gathers[g][number].wait_recv()
        table = jnp.zeros((CY, CX), F32)
        for p in range(16):
            rv, ru = p // 4, p % 4
            offset = ((-ru % 4) * 4 + (-rv % 4)) * 8
            moved = roll_lanes(gath[g, rv, ru, GF].astype(F32), p * 8 - offset)
            table = jnp.where((lanes >> 3) == p, moved, table)
        codes = table.astype(I32)
        for d in range(4):
            w_e, r_e, y_e = codes[d : d + 1], codes[4 + d : 5 + d], codes[8 + d : 9 + d]
            into = (rows_p == jnp.where(y_e > 0, w_e * CY + y_e - 1, -1)).astype(F32).astype(BF16)
            outof = (rows_q == lane_p * CY + r_e).astype(F32).astype(BF16)
            pick[d] = lax.dot_general(into, outof, NT, preferred_element_type=F32).astype(BF16)

        def spread_quarter(d, carry):
            chosen = pick[d]
            for pair in range(GF // 2):
                blocks = jnp.concatenate(
                    [gath[g, :, :, 2 * pair + h].reshape(256, CX) for h in range(2)], axis=1
                )
                summed = jnp.dot(chosen, blocks, preferred_element_type=F32).astype(BF16)
                for h in range(2):
                    for w in range(WTAB):
                        spread[d, w, pl.ds((2 * pair + h) * CY, CY)] = summed[
                            w * CY : (w + 1) * CY, h * CX : (h + 1) * CX
                        ]
            return carry

        lax.fori_loop(0, 4, spread_quarter, 0)
        table_all = jnp.concatenate([weight[w] for w in range(WTAB)], axis=1)
        for d2 in range(2):
            chosen = jnp.concatenate(
                [
                    jnp.concatenate([spread[2 * d2, w], spread[2 * d2 + 1, w]], axis=0)
                    for w in range(WTAB)
                ],
                axis=1,
            )
            result = lax.dot_general(chosen, table_all, NT, preferred_element_type=F32).astype(BF16)
            for h in range(2):
                outgoing[g, 2 * d2 + h] = result[h * 128 : (h + 1) * 128].reshape(GF, CY, CX)
        for d in range(4):
            target = (1 - comp, tile if d == 0 else shifted(q, d))
            copy = remote(
                outgoing.at[g, d], arrived.at[g, (4 - d) % 4], sc_send.at[g, d], sc_recv.at[g, d], target
            )
            copy.start()
            scatters.append(copy)

    edge = (lanes < 4) | (lanes >= CX - 4)

    def solve_field(f, carry):
        m, turn = f >> 3, CX - 4 - 16 * (f & 7)
        solved = jnp.zeros((CY, CX), F32)
        kept = []
        for k in range(LEV):
            value = jnp.where(edge, roll_dynamic(fixed[k * 3 + m], turn), state[k, f])
            solved = solve_coef[0, k] * value + solve_coef[1, k] * solved
            kept.append(solved)
        upper = kept[-1]
        state[LEV - 1, f] = upper
        for k in reversed(range(LEV - 1)):
            upper = kept[k] + solve_coef[2, k] * upper
            state[k, f] = upper
        return carry

    lax.fori_loop(0, FIELDS, solve_field, 0)
    store = pltpu.make_async_copy(state, solved_hbm, store_sem)
    store.start()

    for copy in scatters:
        copy.wait_recv()
    for g in range(GROUPS):
        total = arrived[g, 0].astype(F32)
        for d in range(1, 4):
            total = total + arrived[g, d].astype(F32)
        incoming_ref[g * GF : (g + 1) * GF] = total

    for g in range(GROUPS):
        for copy in gathers[g]:
            copy.wait_send()
    for copy in halos:
        copy.wait_send()
    for copy in scatters:
        copy.wait_send()
    store.wait()


def roll_dynamic(value, shift):
    return pltpu.roll(value, shift, 1)


def per_device(
    state_field,
    courant,
    diffusivity,
    coupling_rate,
    weight_table,
    source_row,
    destination_tile_ids,
    dest_row,
    weight_slot,
):
    vmem, anywhere = pl.BlockSpec(memory_space=pltpu.VMEM), pl.BlockSpec(memory_space=pl.ANY)
    plane = (CY, CX)
    solved, gain, incoming = pl.pallas_call(
        kernel,
        out_shape=(
            jax.ShapeDtypeStruct((LEV, FIELDS) + plane, F32),
            jax.ShapeDtypeStruct((LEV,) + plane, F32),
            jax.ShapeDtypeStruct((FIELDS,) + plane, F32),
        ),
        in_specs=[anywhere, vmem, vmem, vmem, anywhere, vmem, vmem, vmem, vmem],
        out_specs=(anywhere, vmem, vmem),
        scratch_shapes=[
            pltpu.VMEM((LEV, FIELDS) + plane, F32),
            pltpu.VMEM((WTAB, CX, CX), BF16),
            pltpu.VMEM((24,) + plane, F32),
            pltpu.VMEM((2, LEV) + plane, F32),
            pltpu.VMEM((2, 7) + plane, F32),
            pltpu.VMEM((2, 7) + plane, F32),
            pltpu.VMEM((24,) + plane, F32),
            pltpu.VMEM((GROUPS, 4, 4, SLABS) + plane, BF16),
            pltpu.VMEM((4, WTAB * CY, 256), BF16),
            pltpu.VMEM((4, WTAB, GF * CY, CX), BF16),
            pltpu.VMEM((GROUPS, 4, GF) + plane, BF16),
            pltpu.VMEM((GROUPS, 4, GF) + plane, BF16),
            pltpu.VMEM((3, LEV) + plane, F32),
            pltpu.SemaphoreType.DMA((LEV,)),
            pltpu.SemaphoreType.DMA,
            pltpu.SemaphoreType.DMA,
            pltpu.SemaphoreType.DMA((GROUPS, 8)),
            pltpu.SemaphoreType.DMA((GROUPS, 8)),
            pltpu.SemaphoreType.DMA((2,)),
            pltpu.SemaphoreType.DMA((2,)),
            pltpu.SemaphoreType.DMA((GROUPS, 4)),
            pltpu.SemaphoreType.DMA((GROUPS, 4)),
        ],
        compiler_params=pltpu.CompilerParams(
            collective_id=0, has_side_effects=True, vmem_limit_bytes=48 * 2**20
        ),
        name="interval",
    )(
        state_field[0],
        courant[0],
        diffusivity[0],
        coupling_rate[0],
        weight_table,
        source_row[0],
        destination_tile_ids.reshape(1, ENTRIES),
        dest_row[0],
        weight_slot[0],
    )
    return (solved + gain[:, None] * incoming[None])[None]


def solution(mesh):
    return jax.shard_map(
        per_device,
        mesh=mesh,
        in_specs=(
            P("comp", None, None, None, "tile"),
            P("comp", None, None, None, "tile"),
            P("comp", None, None, "tile"),
            P("comp", None, "tile"),
            P(),
            P("comp", "tile", None),
            P("comp", "tile", None, None),
            P("comp", "tile", None),
            P("comp", "tile", None),
        ),
        out_specs=P("comp", None, None, None, "tile"),
        check_vma=False,
    )
```

```python
import jax
import jax.numpy as jnp
from jax import lax
from jax.experimental import pallas as pl
from jax.experimental.pallas import tpu as pltpu
from jax.sharding import PartitionSpec as P

MESH = pl.DeviceIdType.MESH
NT = (((1,), (1,)), ((), ()))
ORDER = (0, 1, 3, 2)
LEV, FIELDS, CY, CX = 8, 24, 16, 128
ENTRIES, WTAB = 384, 32
GROUPS = 3
GF = FIELDS // GROUPS
SLABS = GF + 1
STRIDE = (16, 4, 1)
AXES = ((0, 1, 2), (1, 2, 0), (2, 0, 1))
F32, BF16, I32 = jnp.float32, jnp.bfloat16, jnp.int32


def iota(shape, dim):
    return lax.broadcasted_iota(I32, shape, dim)


def roll_lanes(value, shift):
    return pltpu.roll(value, shift % CX, 1)


def stencil_coefs(cx, cy):
    rows = iota(cx.shape, 0)
    cxp, cxm = jnp.maximum(cx, 0.0), jnp.minimum(cx, 0.0)
    cy = jnp.where(rows < CY - 1, cy, 0.0)
    cyp, cym = jnp.maximum(cy, 0.0), jnp.minimum(cy, 0.0)
    west = roll_lanes(cxp, 1)
    south = pltpu.roll(cyp, 1, 0)
    centre = 1.0 - cxp + roll_lanes(cxm, 1) - cyp + pltpu.roll(cym, 1, 0)
    return centre, -cxm, west, -cym, south


def one_step(a, coefs):
    centre, east, west, north, south = coefs
    return (
        centre * a
        + east * roll_lanes(a, CX - 1)
        + west * roll_lanes(a, 1)
        + north * pltpu.roll(a, CY - 1, 0)
        + south * pltpu.roll(a, 1, 0)
    )


def replicate(value):
    for shift in (16, 32, 64):
        value = value + roll_lanes(value, shift)
    return value


def kernel(
    state_hbm,
    courant_hbm,
    diff_hbm,
    rate_hbm,
    weight_hbm,
    srow_hbm,
    dest_hbm,
    drow_hbm,
    wslot_hbm,
    solved_hbm,
    gain_ref,
    incoming_ref,
    state,
    courant_ref,
    diff_ref,
    rate_ref,
    entries,
    weight,
    packed,
    cpacked,
    strips,
    strip_coef,
    halo_out,
    halo_in,
    coef,
    gath,
    pick,
    spread,
    outgoing,
    arrived,
    solve_coef,
    load_sem,
    entry_sem,
    small_sem,
    store_sem,
    ag_send,
    ag_recv,
    halo_send,
    halo_recv,
    sc_send,
    sc_recv,
):
    comp, tile = lax.axis_index("comp"), lax.axis_index("tile")
    coords = (tile >> 4, (tile >> 2) & 3, tile & 3)

    def shifted(axis, step):
        return tile + (((coords[axis] + step) & 3) - coords[axis]) * STRIDE[axis]

    right, left = (tile + 1) & 63, (tile + 63) & 63
    barrier = pltpu.get_barrier_semaphore()
    greeted = [(comp, shifted(axis, step)) for axis in range(3) for step in (1, 3)]
    greeted += [(comp, right), (comp, left), (1 - comp, tile)]
    greeted += [(1 - comp, shifted(axis, step)) for axis in range(3) for step in (1, 2, 3)]
    for target in greeted:
        pl.semaphore_signal(barrier, inc=1, device_id=target, device_id_type=MESH)

    loads = [
        pltpu.make_async_copy(state_hbm.at[k], state.at[k], load_sem.at[k]) for k in range(LEV)
    ]
    entry_loads = [
        pltpu.make_async_copy(source, entries.at[pl.ds(n, 1)], entry_sem.at[n])
        for n, source in enumerate((dest_hbm, srow_hbm, drow_hbm, wslot_hbm))
    ]
    small_loads = [
        pltpu.make_async_copy(source, target, small_sem.at[n])
        for n, (source, target) in enumerate(
            ((courant_hbm, courant_ref), (diff_hbm, diff_ref), (rate_hbm, rate_ref), (weight_hbm, weight))
        )
    ]
    loads[0].start()
    for load in entry_loads:
        load.start()
    small_loads[0].start()
    for load in loads[1:]:
        load.start()
    for load in small_loads[1:]:
        load.start()

    for load in entry_loads:
        load.wait()
    targets, srow, drow, wslot = (entries[n : n + 1] for n in range(4))
    named = (iota((64, ENTRIES), 0) == targets).astype(F32)
    before = (iota((ENTRIES, ENTRIES), 0) < iota((ENTRIES, ENTRIES), 1)).astype(F32)
    counts = jnp.dot(named.astype(BF16), before.astype(BF16), preferred_element_type=F32)
    rank = jnp.sum(named * counts, axis=0, keepdims=True).astype(I32)
    rel = (
        ((targets >> 4) - coords[0]) & 3,
        ((targets >> 2) - coords[1]) & 3,
        (targets - coords[2]) & 3,
    )
    kind, quarter = iota((16, ENTRIES), 0) >> 2, iota((16, ENTRIES), 0) & 3
    values = jnp.where(kind == 0, wslot, jnp.where(kind == 1, srow, drow + 1))
    for g, (u, v, q) in enumerate(AXES):
        spot = (rel[u] * 4 + rel[v]) * 8 + rank
        hot = (iota((CX, ENTRIES), 0) == spot).astype(F32).astype(BF16)
        kept = jnp.where((quarter == rel[q]) & (kind < 3), values, 0)
        table = lax.dot_general(kept.astype(F32).astype(BF16), hot, NT, preferred_element_type=F32)
        gath[g, 0, 0, GF] = table.astype(BF16)

    loads[0].wait()
    for g in range(GROUPS):
        gath[g, 0, 0, :GF] = state[0, g * GF : (g + 1) * GF].astype(BF16)

    pl.semaphore_wait(barrier, len(greeted))

    def remote(src, dst, send, recv, target):
        return pltpu.make_async_remote_copy(
            src_ref=src,
            dst_ref=dst,
            send_sem=send,
            recv_sem=recv,
            device_id=target,
            device_id_type=MESH,
        )

    def gather_copy(g, number):
        u, v, q = AXES[g]
        block = lambda i, j: gath.at[g, i, j]
        low, high = pl.ds(0, 5), pl.ds(5, SLABS - 5)
        src, dst, axis, step = (
            (block(0, 0), block(0, 2), u, 1),
            (block(0, 0), block(0, 1), u, 3),
            (block(0, 0), block(2, 0), v, 1),
            (block(0, 0), block(1, 0), v, 3),
            (gath.at[g, 0, 2, low], gath.at[g, 0, 3, low], u, 1),
            (gath.at[g, 0, 1, high], gath.at[g, 0, 3, high], u, 3),
            (gath.at[g, 0, pl.ds(1, 2)], gath.at[g, 2, pl.ds(1, 2)], v, 1),
            (gath.at[g, 0, pl.ds(1, 2)], gath.at[g, 1, pl.ds(1, 2)], v, 3),
            (block(2, 0), block(3, 0), v, 1),
            (block(0, 3), block(2, 3), v, 1),
            (block(0, 3), block(1, 3), v, 3),
            (block(2, 1), block(3, 1), v, 1),
            (block(1, 2), block(3, 2), v, 3),
            (block(1, 3), block(3, 3), v, 3),
        )[number]
        return remote(src, dst, ag_send.at[g, number], ag_recv.at[g, number], (comp, shifted(axis, step)))

    gathers = [[gather_copy(g, number) for number in range(14)] for g in range(GROUPS)]
    rounds = ((0, 1, 2, 3), (4, 5, 6, 7, 8), (9, 10, 11, 12), (13,))

    def start_round(n):
        for number in rounds[n]:
            for g in range(GROUPS):
                gathers[g][number].start()

    def wait_round(n):
        for number in rounds[n]:
            for g in range(GROUPS):
                gathers[g][number].wait_recv()

    start_round(0)

    for load in loads[1:]:
        load.wait()
    small_loads[0].wait()
    lanes = iota((CY, CX), 1)
    group_of, place = lanes >> 4, lanes & 15

    def pack_level(k, carry):
        for m in range(3):
            value = roll_lanes(state[k, m * 8], 8)
            for i in range(1, 8):
                value = jnp.where(group_of == i, roll_lanes(state[k, m * 8 + i], 16 * i + 8), value)
            packed[k * 3 + m] = value
        return carry

    lax.fori_loop(0, LEV, pack_level, 0)
    planes = [(c, k) for c in range(2) for k in range(LEV)]
    for c, k in planes:
        cpacked[c, k] = replicate(jnp.where(lanes < 16, roll_lanes(courant_ref[c, k], 8), 0.0))
    quad = (lanes >> 2) & 3
    for n in range(6):
        for side, base in ((0, 4), (1, 8)):
            value = roll_lanes(packed[4 * n], -base)
            for t in range(1, 4):
                value = jnp.where(quad == t, roll_lanes(packed[4 * n + t], 4 * t - base), value)
            halo_out[side, n] = value
    for side, base in ((0, 4), (1, 8)):
        value = roll_lanes(cpacked[0, 0], -base)
        for e in range(1, 16):
            moved = roll_lanes(cpacked[e // 8, e % 8], 4 * (e % 4) - base)
            value = jnp.where((lanes >> 2) == e, moved, value)
        halo_out[side, 6] = value
    halos = [
        remote(halo_out.at[side], halo_in.at[side], halo_send.at[side], halo_recv.at[side], (comp, target))
        for side, target in ((0, right), (1, left))
    ]
    for copy in halos:
        copy.start()

    wait_round(0)
    start_round(1)

    def coef_level(k, carry):
        for n, value in enumerate(stencil_coefs(courant_ref[0, k], courant_ref[1, k])):
            coef[k, n] = value
        return carry

    for k in range(LEV):
        coef_level(k, 0)

    def transport_step(n, carry):
        k = n >> 2
        coefs = [coef[k, n] for n in range(5)]
        for f in range(FIELDS):
            state[k, f] = one_step(state[k, f], coefs)
        return carry

    lax.fori_loop(0, 4, transport_step, 0)
    wait_round(1)
    start_round(2)
    lax.fori_loop(4, 16, transport_step, 0)
    wait_round(2)
    start_round(3)
    lax.fori_loop(16, 32, transport_step, 0)

    small_loads[3].wait()
    wait_round(3)
    rows_p, rows_q = iota((WTAB * CY, CX), 0), iota((256, CX), 0)
    lane_p = iota((1, CX), 1) >> 3
    scatters = []
    for g, (u, v, q) in enumerate(AXES):
        table = jnp.zeros((CY, CX), F32)
        for p in range(16):
            rv, ru = ORDER[p // 4], ORDER[p % 4]
            offset = ((-ru % 4) * 4 + (-rv % 4)) * 8
            moved = roll_lanes(gath[g, p // 4, p % 4, GF].astype(F32), p * 8 - offset)
            table = jnp.where((lanes >> 3) == p, moved, table)
        codes = table.astype(I32)
        for d in range(4):
            w_e, r_e, y_e = codes[d : d + 1], codes[4 + d : 5 + d], codes[8 + d : 9 + d]
            into = (rows_p == jnp.where(y_e > 0, w_e * CY + y_e - 1, -1)).astype(F32).astype(BF16)
            outof = (rows_q == lane_p * CY + r_e).astype(F32).astype(BF16)
            pick[d] = lax.dot_general(into, outof, NT, preferred_element_type=F32).astype(BF16)

        def spread_quarter(d, carry):
            chosen = pick[d]
            for pair in range(GF // 2):
                blocks = jnp.concatenate(
                    [gath[g, :, :, 2 * pair + h].reshape(256, CX) for h in range(2)], axis=1
                )
                summed = jnp.dot(chosen, blocks, preferred_element_type=F32).astype(BF16)
                for h in range(2):
                    for w in range(WTAB):
                        spread[d, w, pl.ds((2 * pair + h) * CY, CY)] = summed[
                            w * CY : (w + 1) * CY, h * CX : (h + 1) * CX
                        ]
            return carry

        lax.fori_loop(0, 4, spread_quarter, 0)
        table_all = jnp.concatenate([weight[w] for w in range(WTAB)], axis=1)
        for d2 in range(2):
            chosen = jnp.concatenate(
                [
                    jnp.concatenate([spread[2 * d2, w], spread[2 * d2 + 1, w]], axis=0)
                    for w in range(WTAB)
                ],
                axis=1,
            )
            result = lax.dot_general(chosen, table_all, NT, preferred_element_type=F32).astype(BF16)
            for h in range(2):
                outgoing[g, 2 * d2 + h] = result[h * 128 : (h + 1) * 128].reshape(GF, CY, CX)
        for d in range(4):
            target = (1 - comp, tile if d == 0 else shifted(q, d))
            copy = remote(
                outgoing.at[g, d], arrived.at[g, (4 - d) % 4], sc_send.at[g, d], sc_recv.at[g, d], target
            )
            copy.start()
            scatters.append(copy)

    small_loads[1].wait()
    small_loads[2].wait()
    ratio = jnp.zeros((CY, CX), F32)
    gain = None
    gains, ratios = [], []
    for k in range(LEV):
        above = diff_ref[k] if k < LEV - 1 else jnp.zeros((CY, CX), F32)
        below = diff_ref[k - 1] if k > 0 else jnp.zeros((CY, CX), F32)
        inverse = 1.0 / (1.0 + below + above - below * ratio)
        ratio = above * inverse
        solve_coef[0, k] = inverse
        solve_coef[1, k] = below * inverse
        solve_coef[2, k] = ratio
        gain = inverse if k == 0 else below * inverse * gain
        gains.append(gain)
        ratios.append(ratio)
    value = jnp.zeros((CY, CX), F32)
    for k in reversed(range(LEV)):
        value = gains[k] + ratios[k] * value
        gain_ref[k] = value * rate_ref[...]

    for copy in halos:
        copy.wait_recv()
    mid = (place >= 8) & (place < 12)
    sides = ([], [])
    for c, k in planes:
        e = c * 8 + k
        own = cpacked[c, k]
        from_left = replicate(jnp.where(lanes < 4, roll_lanes(halo_in[0, 6], -4 * e), 0.0))
        from_right = replicate(jnp.where(mid & (lanes < 16), roll_lanes(halo_in[1, 6], 8 - 4 * e), 0.0))
        strip_coef[0, k >> 2, k & 3, c] = jnp.where(place < 4, from_left, roll_lanes(own, -4))
        strip_coef[1, k >> 2, k & 3, c] = jnp.where(mid, from_right, own)
    for k in range(LEV):
        for side in range(2):
            held = strip_coef.at[side, k >> 2, k & 3]
            for n, value in enumerate(stencil_coefs(held[0], held[1])):
                held[n] = value

    for p in range(3 * LEV):
        n, t = p >> 2, p & 3
        own = packed[p]
        strips[0, p // 12, p % 12] = jnp.where(
            place < 4, roll_lanes(halo_in[0, n], -4 * t), roll_lanes(own, -4)
        )
        strips[1, p // 12, p % 12] = jnp.where(mid, roll_lanes(halo_in[1, n], 8 - 4 * t), own)

    def strip_step(n, carry):
        half = n >> 2
        for j in range(4):
            for side in range(2):
                coefs = [strip_coef[side, half, j, i] for i in range(5)]
                for m in range(3):
                    p = j * 3 + m
                    strips[side, half, p] = one_step(strips[side, half, p], coefs)
        return carry

    lax.fori_loop(0, 8, strip_step, 0)
    for p in range(3 * LEV):
        h, r = p // 12, p % 12
        packed[p] = jnp.where(place < 4, roll_lanes(strips[1, h, r], -4), strips[0, h, r])

    edge = (lanes < 4) | (lanes >= CX - 4)

    def solve_fields(n, carry):
        m = n >> 1
        for j in range(4):
            f = n * 4 + j
            turn = CX - 4 - 16 * ((n & 1) * 4 + j)
            solved = jnp.zeros((CY, CX), F32)
            kept = []
            for k in range(LEV):
                value = jnp.where(edge, pltpu.roll(packed[k * 3 + m], turn, 1), state[k, f])
                solved = solve_coef[0, k] * value + solve_coef[1, k] * solved
                kept.append(solved)
            upper = kept[-1]
            state[LEV - 1, f] = upper
            for k in reversed(range(LEV - 1)):
                upper = kept[k] + solve_coef[2, k] * upper
                state[k, f] = upper
        return carry

    lax.fori_loop(0, FIELDS // 4, solve_fields, 0)
    store = pltpu.make_async_copy(state, solved_hbm, store_sem)
    store.start()

    for copy in scatters:
        copy.wait_recv()
    for g in range(GROUPS):
        total = arrived[g, 0].astype(F32)
        for d in range(1, 4):
            total = total + arrived[g, d].astype(F32)
        incoming_ref[g * GF : (g + 1) * GF] = total

    for g in range(GROUPS):
        for copy in gathers[g]:
            copy.wait_send()
    for copy in halos:
        copy.wait_send()
    for copy in scatters:
        copy.wait_send()
    store.wait()


def per_device(
    state_field,
    courant,
    diffusivity,
    coupling_rate,
    weight_table,
    source_row,
    destination_tile_ids,
    dest_row,
    weight_slot,
):
    vmem, hbm = pl.BlockSpec(memory_space=pltpu.VMEM), pl.BlockSpec(memory_space=pltpu.HBM)
    plane = (CY, CX)
    solved, gain, incoming = pl.pallas_call(
        kernel,
        out_shape=(
            jax.ShapeDtypeStruct((LEV, FIELDS) + plane, F32),
            jax.ShapeDtypeStruct((LEV,) + plane, F32),
            jax.ShapeDtypeStruct((FIELDS,) + plane, F32),
        ),
        in_specs=[hbm] * 9,
        out_specs=(hbm, vmem, vmem),
        scratch_shapes=[
            pltpu.VMEM((LEV, FIELDS) + plane, F32),
            pltpu.VMEM((2, LEV) + plane, F32),
            pltpu.VMEM((LEV,) + plane, F32),
            pltpu.VMEM(plane, F32),
            pltpu.VMEM((4, ENTRIES), I32),
            pltpu.VMEM((WTAB, CX, CX), BF16),
            pltpu.VMEM((24,) + plane, F32),
            pltpu.VMEM((2, LEV) + plane, F32),
            pltpu.VMEM((2, 2, 12) + plane, F32),
            pltpu.VMEM((2, 2, 4, 5) + plane, F32),
            pltpu.VMEM((2, 7) + plane, F32),
            pltpu.VMEM((2, 7) + plane, F32),
            pltpu.VMEM((LEV, 5) + plane, F32),
            pltpu.VMEM((GROUPS, 4, 4, SLABS) + plane, BF16),
            pltpu.VMEM((4, WTAB * CY, 256), BF16),
            pltpu.VMEM((4, WTAB, GF * CY, CX), BF16),
            pltpu.VMEM((GROUPS, 4, GF) + plane, BF16),
            pltpu.VMEM((GROUPS, 4, GF) + plane, BF16),
            pltpu.VMEM((3, LEV) + plane, F32),
            pltpu.SemaphoreType.DMA((LEV,)),
            pltpu.SemaphoreType.DMA((4,)),
            pltpu.SemaphoreType.DMA((4,)),
            pltpu.SemaphoreType.DMA,
            pltpu.SemaphoreType.DMA((GROUPS, 14)),
            pltpu.SemaphoreType.DMA((GROUPS, 14)),
            pltpu.SemaphoreType.DMA((2,)),
            pltpu.SemaphoreType.DMA((2,)),
            pltpu.SemaphoreType.DMA((GROUPS, 4)),
            pltpu.SemaphoreType.DMA((GROUPS, 4)),
        ],
        compiler_params=pltpu.CompilerParams(
            collective_id=0, has_side_effects=True, vmem_limit_bytes=60 * 2**20
        ),
        name="interval",
    )(
        state_field[0],
        courant[0],
        diffusivity[0],
        coupling_rate[0],
        weight_table,
        source_row[0],
        destination_tile_ids.reshape(1, ENTRIES),
        dest_row[0],
        weight_slot[0],
    )
    return (solved + gain[:, None] * incoming[None])[None]


def solution(mesh):
    return jax.shard_map(
        per_device,
        mesh=mesh,
        in_specs=(
            P("comp", None, None, None, "tile"),
            P("comp", None, None, None, "tile"),
            P("comp", None, None, "tile"),
            P("comp", None, "tile"),
            P(),
            P("comp", "tile", None),
            P("comp", "tile", None, None),
            P("comp", "tile", None),
            P("comp", "tile", None),
        ),
        out_specs=P("comp", None, None, None, "tile"),
        check_vma=False,
    )
```

```python
import jax
import jax.numpy as jnp
from jax import lax
from jax.experimental import pallas as pl
from jax.experimental.pallas import tpu as pltpu
from jax.sharding import PartitionSpec as P

MESH = pl.DeviceIdType.MESH
NT = (((1,), (1,)), ((), ()))
ORDER = (0, 1, 3, 2)
LEV, FIELDS, CY, CX = 8, 24, 16, 128
ENTRIES, WTAB = 384, 32
GROUPS = 3
GF = FIELDS // GROUPS
HALF = GF // 2
SLABS = HALF + 1
AXES = ((0, 1, 2), (1, 2, 0), (2, 0, 1))
F32, BF16, I32 = jnp.float32, jnp.bfloat16, jnp.int32


def iota(shape, dim):
    return lax.broadcasted_iota(I32, shape, dim)


def roll_lanes(value, shift):
    return pltpu.roll(value, shift % CX, 1)


def stencil_coefs(cx, cy):
    rows = iota(cx.shape, 0)
    cxp, cxm = jnp.maximum(cx, 0.0), jnp.minimum(cx, 0.0)
    cy = jnp.where(rows < CY - 1, cy, 0.0)
    cyp, cym = jnp.maximum(cy, 0.0), jnp.minimum(cy, 0.0)
    west = roll_lanes(cxp, 1)
    south = pltpu.roll(cyp, 1, 0)
    centre = 1.0 - cxp + roll_lanes(cxm, 1) - cyp + pltpu.roll(cym, 1, 0)
    return centre, -cxm, west, -cym, south


def one_step(a, coefs):
    centre, east, west, north, south = coefs
    return (
        centre * a
        + east * roll_lanes(a, CX - 1)
        + west * roll_lanes(a, 1)
        + north * pltpu.roll(a, CY - 1, 0)
        + south * pltpu.roll(a, 1, 0)
    )


def replicate(value):
    for shift in (16, 32, 64):
        value = value + roll_lanes(value, shift)
    return value


def kernel(
    state_hbm,
    courant_hbm,
    diff_hbm,
    rate_hbm,
    weight_hbm,
    srow_hbm,
    dest_hbm,
    drow_hbm,
    wslot_hbm,
    solved_hbm,
    gain_ref,
    incoming_ref,
    state,
    courant_ref,
    diff_ref,
    rate_ref,
    entries,
    weight,
    packed,
    cpacked,
    strips,
    strip_coef,
    halo_out,
    halo_in,
    coef,
    gath,
    pick,
    spread,
    outgoing,
    arrived,
    solve_coef,
    load_sem,
    entry_sem,
    small_sem,
    store_sem,
    ag_send,
    ag_recv,
    halo_send,
    halo_recv,
    sc_send,
    sc_recv,
):
    comp, tile = lax.axis_index("comp"), lax.axis_index("tile")
    coords = (tile >> 4, (tile >> 2) & 3, tile & 3)

    def shifted(axis, step):
        place = 4 - 2 * axis
        here = (tile >> place) & 3
        return tile + ((((here + step) & 3) - here) << place)

    right, left = (tile + 1) & 63, (tile + 63) & 63
    barrier = pltpu.get_barrier_semaphore()
    greeted = [(comp, shifted(axis, step)) for axis in range(3) for step in (1, 3)]
    greeted += [(comp, right), (comp, left), (1 - comp, tile)]
    greeted += [(1 - comp, shifted(axis, step)) for axis in range(3) for step in (1, 2, 3)]
    for target in greeted:
        pl.semaphore_signal(barrier, inc=1, device_id=target, device_id_type=MESH)

    loads = [
        pltpu.make_async_copy(state_hbm.at[k], state.at[k], load_sem.at[k]) for k in range(LEV)
    ]
    entry_loads = [
        pltpu.make_async_copy(source, entries.at[pl.ds(n, 1)], entry_sem.at[n])
        for n, source in enumerate((dest_hbm, srow_hbm, drow_hbm, wslot_hbm))
    ]
    small_loads = [
        pltpu.make_async_copy(source, target, small_sem.at[n])
        for n, (source, target) in enumerate(
            ((courant_hbm, courant_ref), (diff_hbm, diff_ref), (rate_hbm, rate_ref), (weight_hbm, weight))
        )
    ]
    loads[0].start()
    for load in entry_loads:
        load.start()
    small_loads[0].start()
    for load in loads[1:]:
        load.start()
    for load in small_loads[1:]:
        load.start()

    for load in entry_loads:
        load.wait()
    targets, srow, drow, wslot = (entries[n : n + 1] for n in range(4))
    named = (iota((64, ENTRIES), 0) == targets).astype(F32)
    before = (iota((ENTRIES, ENTRIES), 0) < iota((ENTRIES, ENTRIES), 1)).astype(F32)
    counts = jnp.dot(named.astype(BF16), before.astype(BF16), preferred_element_type=F32)
    rank = jnp.sum(named * counts, axis=0, keepdims=True).astype(I32)
    rel = (
        ((targets >> 4) - coords[0]) & 3,
        ((targets >> 2) - coords[1]) & 3,
        (targets - coords[2]) & 3,
    )
    kind, quarter = iota((16, ENTRIES), 0) >> 2, iota((16, ENTRIES), 0) & 3
    values = jnp.where(kind == 0, wslot, jnp.where(kind == 1, srow, drow + 1))
    for g, (u, v, q) in enumerate(AXES):
        spot = (rel[u] * 4 + rel[v]) * 8 + rank
        hot = (iota((CX, ENTRIES), 0) == spot).astype(F32).astype(BF16)
        kept = jnp.where((quarter == rel[q]) & (kind < 3), values, 0)
        table = lax.dot_general(kept.astype(F32).astype(BF16), hot, NT, preferred_element_type=F32)
        gath[0, g, 0, 0, HALF] = table.astype(BF16)

    loads[0].wait()
    for h in range(2):
        for g in range(GROUPS):
            start = (g * 2 + h) * HALF
            gath[h, g, 0, 0, :HALF] = state[0, start : start + HALF].astype(BF16)

    pl.semaphore_wait(barrier, len(greeted))

    def remote(src, dst, send, recv, target):
        return pltpu.make_async_remote_copy(
            src_ref=src,
            dst_ref=dst,
            send_sem=send,
            recv_sem=recv,
            device_id=target,
            device_id_type=MESH,
        )

    def gather_copy(h, g, number):
        slabs = SLABS - h
        cut = 3 - h
        every, low, high = pl.ds(0, slabs), pl.ds(0, cut), pl.ds(cut, slabs - cut)
        block = lambda i, j, part=every: gath.at[h, g, i, j, part]
        u, v = g, (g + 1) % 3
        src, dst, axis, step = (
            (block(0, 0), block(0, 2), u, 1),
            (block(0, 0), block(0, 1), u, 3),
            (block(0, 0), block(2, 0), v, 1),
            (block(0, 0), block(1, 0), v, 3),
            (block(0, 2, low), block(0, 3, low), u, 1),
            (block(0, 1, high), block(0, 3, high), u, 3),
            (block(0, pl.ds(1, 2)), block(2, pl.ds(1, 2)), v, 1),
            (block(0, pl.ds(1, 2)), block(1, pl.ds(1, 2)), v, 3),
            (block(2, 0), block(3, 0), v, 1),
            (block(0, 3), block(2, 3), v, 1),
            (block(0, 3), block(1, 3), v, 3),
            (block(2, 1), block(3, 1), v, 1),
            (block(1, 2), block(3, 2), v, 3),
            (block(1, 3), block(3, 3), v, 3),
        )[number]
        return remote(
            src, dst, ag_send.at[h, g, number], ag_recv.at[h, g, number], (comp, shifted(axis, step))
        )

    def after(h, g, *moves):
        for waited, started in moves:
            for number in waited:
                gather_copy(h, g, number).wait_recv()
            for number in started:
                gather_copy(h, g, number).start()

    first = (((), (0, 1, 2, 3)),)
    second = (((0, 1), (4, 5, 6, 7)), ((2,), (8,)))
    third = (((4, 5), (9, 10)), ((6,), (11,)), ((7,), (12,)))
    fourth = (((10,), (13,)),)
    rest = (((3, 8, 9, 11, 12, 13), ()),)

    for g in range(GROUPS):
        after(0, g, *first)

    for load in loads[1:]:
        load.wait()
    small_loads[0].wait()
    lanes = iota((CY, CX), 1)
    group_of, place = lanes >> 4, lanes & 15

    def pack_level(k, carry):
        for m in range(3):
            value = roll_lanes(state[k, m * 8], 8)
            for i in range(1, 8):
                value = jnp.where(group_of == i, roll_lanes(state[k, m * 8 + i], 16 * i + 8), value)
            packed[k * 3 + m] = value
        return carry

    lax.fori_loop(0, LEV, pack_level, 0)
    planes = [(c, k) for c in range(2) for k in range(LEV)]
    for c, k in planes:
        cpacked[c, k] = replicate(jnp.where(lanes < 16, roll_lanes(courant_ref[c, k], 8), 0.0))
    quad = (lanes >> 2) & 3
    for n in range(6):
        for side, base in ((0, 4), (1, 8)):
            value = roll_lanes(packed[4 * n], -base)
            for t in range(1, 4):
                value = jnp.where(quad == t, roll_lanes(packed[4 * n + t], 4 * t - base), value)
            halo_out[side, n] = value
    for side, base in ((0, 4), (1, 8)):
        value = roll_lanes(cpacked[0, 0], -base)
        for e in range(1, 16):
            moved = roll_lanes(cpacked[e // 8, e % 8], 4 * (e % 4) - base)
            value = jnp.where((lanes >> 2) == e, moved, value)
        halo_out[side, 6] = value
    halos = [
        remote(halo_out.at[side], halo_in.at[side], halo_send.at[side], halo_recv.at[side], (comp, target))
        for side, target in ((0, right), (1, left))
    ]
    for copy in halos:
        copy.start()

    for g in range(GROUPS):
        after(0, g, *second)
    for g in range(GROUPS):
        after(1, g, *first)

    def level_coefs(k, carry):
        for n, value in enumerate(stencil_coefs(courant_ref[0, k], courant_ref[1, k])):
            coef[k, n] = value
        return carry

    for k in range(LEV):
        level_coefs(k, 0)

    for copy in halos:
        copy.wait_recv()
    mid = (place >= 8) & (place < 12)
    for c, k in planes:
        e = c * 8 + k
        own = cpacked[c, k]
        from_left = replicate(jnp.where(lanes < 4, roll_lanes(halo_in[0, 6], -4 * e), 0.0))
        from_right = replicate(jnp.where(mid & (lanes < 16), roll_lanes(halo_in[1, 6], 8 - 4 * e), 0.0))
        strip_coef[0, k >> 2, k & 3, c] = jnp.where(place < 4, from_left, roll_lanes(own, -4))
        strip_coef[1, k >> 2, k & 3, c] = jnp.where(mid, from_right, own)

    for g in range(GROUPS):
        after(0, g, *third)
    for g in range(GROUPS):
        after(1, g, *second)

    for k in range(LEV):
        for side in range(2):
            held = strip_coef.at[side, k >> 2, k & 3]
            for n, value in enumerate(stencil_coefs(held[0], held[1])):
                held[n] = value
    for p in range(3 * LEV):
        n, t = p >> 2, p & 3
        own = packed[p]
        strips[0, p // 12, p % 12] = jnp.where(
            place < 4, roll_lanes(halo_in[0, n], -4 * t), roll_lanes(own, -4)
        )
        strips[1, p // 12, p % 12] = jnp.where(mid, roll_lanes(halo_in[1, n], 8 - 4 * t), own)

    for g in range(GROUPS):
        after(0, g, *fourth)

    def strip_step(n, carry):
        half = n >> 2
        for j in range(4):
            for side in range(2):
                coefs = [strip_coef[side, half, j, i] for i in range(5)]
                for m in range(3):
                    p = j * 3 + m
                    strips[side, half, p] = one_step(strips[side, half, p], coefs)
        return carry

    lax.fori_loop(0, 8, strip_step, 0)
    for p in range(3 * LEV):
        i, r = p // 12, p % 12
        packed[p] = jnp.where(place < 4, roll_lanes(strips[1, i, r], -4), strips[0, i, r])

    def transport_step(n, carry):
        k = n >> 2
        coefs = [coef[k, i] for i in range(5)]
        for f in range(FIELDS):
            state[k, f] = one_step(state[k, f], coefs)
        return carry

    def transport_level(k):
        coefs = [coef[k, i] for i in range(5)]
        for step in range(4):
            for f in range(FIELDS):
                state[k, f] = one_step(state[k, f], coefs)

    small_loads[3].wait()
    rows_p, rows_q = iota((WTAB * CY, CX), 0), iota((256, CX), 0)
    lane_p = iota((1, CX), 1) >> 3

    def scatter_copy(h, g, d):
        target = (1 - comp, tile if d == 0 else shifted((g + 2) % 3, d))
        return remote(
            outgoing.at[h, g, d],
            arrived.at[h, g, (4 - d) % 4],
            sc_send.at[h, g, d],
            sc_recv.at[h, g, d],
            target,
        )

    def remap(h, g, carry):
        after(h, g, *rest)
        if h == 0:
            after(1, g, *third)
            table = jnp.zeros((CY, CX), F32)
            for p in range(16):
                rv, ru = ORDER[p // 4], ORDER[p % 4]
                offset = ((-ru % 4) * 4 + (-rv % 4)) * 8
                moved = roll_lanes(gath[0, g, p // 4, p % 4, HALF].astype(F32), p * 8 - offset)
                table = jnp.where((lanes >> 3) == p, moved, table)
            codes = table.astype(I32)
            for d in range(4):
                w_e, r_e, y_e = codes[d : d + 1], codes[4 + d : 5 + d], codes[8 + d : 9 + d]
                into = (rows_p == jnp.where(y_e > 0, w_e * CY + y_e - 1, -1)).astype(F32).astype(BF16)
                outof = (rows_q == lane_p * CY + r_e).astype(F32).astype(BF16)
                pick[g, d] = lax.dot_general(into, outof, NT, preferred_element_type=F32).astype(BF16)
        blocks = [
            jnp.concatenate(
                [gath[h, g, :, :, 2 * pair + i].reshape(256, CX) for i in range(2)], axis=1
            )
            for pair in range(HALF // 2)
        ]
        for d in range(4):
            for pair in range(HALF // 2):
                summed = jnp.dot(pick[g, d], blocks[pair], preferred_element_type=F32).astype(BF16)
                for i in range(2):
                    for w in range(WTAB):
                        row = (d * HALF + 2 * pair + i) * CY
                        spread[w, row : row + CY] = summed[w * CY : (w + 1) * CY, i * CX : (i + 1) * CX]
        transport_level(3 * h + g)
        if h == 0:
            after(1, g, *fourth)
        table_all = jnp.concatenate([weight[w] for w in range(WTAB)], axis=1)
        chosen = jnp.concatenate([spread[w] for w in range(WTAB)], axis=1)
        result = lax.dot_general(chosen, table_all, NT, preferred_element_type=F32).astype(BF16)
        for d in range(4):
            rows = HALF * CY
            outgoing[h, g, d] = result[d * rows : (d + 1) * rows].reshape(HALF, CY, CX)
        for d in range(4):
            scatter_copy(h, g, d).start()
        return carry

    for h in range(2):
        lax.fori_loop(0, GROUPS, lambda g, carry, h=h: remap(h, g, carry), 0)
    lax.fori_loop(24, 32, transport_step, 0)

    small_loads[1].wait()
    small_loads[2].wait()
    ratio = jnp.zeros((CY, CX), F32)
    gain = None
    gains, ratios = [], []
    for k in range(LEV):
        above = diff_ref[k] if k < LEV - 1 else jnp.zeros((CY, CX), F32)
        below = diff_ref[k - 1] if k > 0 else jnp.zeros((CY, CX), F32)
        inverse = 1.0 / (1.0 + below + above - below * ratio)
        ratio = above * inverse
        solve_coef[0, k] = inverse
        solve_coef[1, k] = below * inverse
        solve_coef[2, k] = ratio
        gain = inverse if k == 0 else below * inverse * gain
        gains.append(gain)
        ratios.append(ratio)
    value = jnp.zeros((CY, CX), F32)
    for k in reversed(range(LEV)):
        value = gains[k] + ratios[k] * value
        gain_ref[k] = value * rate_ref[...]

    edge = (lanes < 4) | (lanes >= CX - 4)

    def solve_fields(n, carry):
        m = n >> 1
        for j in range(4):
            f = n * 4 + j
            turn = CX - 4 - 16 * ((n & 1) * 4 + j)
            solved = jnp.zeros((CY, CX), F32)
            kept = []
            for k in range(LEV):
                value = jnp.where(edge, pltpu.roll(packed[k * 3 + m], turn, 1), state[k, f])
                solved = solve_coef[0, k] * value + solve_coef[1, k] * solved
                kept.append(solved)
            upper = kept[-1]
            state[LEV - 1, f] = upper
            for k in reversed(range(LEV - 1)):
                upper = kept[k] + solve_coef[2, k] * upper
                state[k, f] = upper
        return carry

    lax.fori_loop(0, FIELDS // 4, solve_fields, 0)
    store = pltpu.make_async_copy(state, solved_hbm, store_sem)
    store.start()

    for h in range(2):
        for g in range(GROUPS):
            for d in range(4):
                scatter_copy(h, g, d).wait_recv()
            total = arrived[h, g, 0].astype(F32)
            for d in range(1, 4):
                total = total + arrived[h, g, d].astype(F32)
            start = (g * 2 + h) * HALF
            incoming_ref[start : start + HALF] = total

    def finish(g, carry):
        for h in range(2):
            for number in range(14):
                gather_copy(h, g, number).wait_send()
            for d in range(4):
                scatter_copy(h, g, d).wait_send()
        return carry

    lax.fori_loop(0, GROUPS, finish, 0)
    for copy in halos:
        copy.wait_send()
    store.wait()


def combine(solved_hbm, gain_ref, incoming_ref, out_hbm, held, load_sem, store_sem):
    loads = [pltpu.make_async_copy(solved_hbm.at[k], held.at[k], load_sem.at[k]) for k in range(LEV)]
    stores = [pltpu.make_async_copy(held.at[k], out_hbm.at[k], store_sem.at[k]) for k in range(LEV)]
    for load in loads:
        load.start()
    for k in range(LEV):
        loads[k].wait()
        gain = gain_ref[k]
        for f in range(FIELDS):
            held[k, f] = held[k, f] + gain * incoming_ref[f]
        stores[k].start()
    for store in stores:
        store.wait()


def per_device(
    state_field,
    courant,
    diffusivity,
    coupling_rate,
    weight_table,
    source_row,
    destination_tile_ids,
    dest_row,
    weight_slot,
):
    vmem, hbm = pl.BlockSpec(memory_space=pltpu.VMEM), pl.BlockSpec(memory_space=pltpu.HBM)
    plane = (CY, CX)
    solved, gain, incoming = pl.pallas_call(
        kernel,
        out_shape=(
            jax.ShapeDtypeStruct((LEV, FIELDS) + plane, F32),
            jax.ShapeDtypeStruct((LEV,) + plane, F32),
            jax.ShapeDtypeStruct((FIELDS,) + plane, F32),
        ),
        in_specs=[hbm] * 9,
        out_specs=(hbm, vmem, vmem),
        scratch_shapes=[
            pltpu.VMEM((LEV, FIELDS) + plane, F32),
            pltpu.VMEM((2, LEV) + plane, F32),
            pltpu.VMEM((LEV,) + plane, F32),
            pltpu.VMEM(plane, F32),
            pltpu.VMEM((4, ENTRIES), I32),
            pltpu.VMEM((WTAB, CX, CX), BF16),
            pltpu.VMEM((24,) + plane, F32),
            pltpu.VMEM((2, LEV) + plane, F32),
            pltpu.VMEM((2, 2, 12) + plane, F32),
            pltpu.VMEM((2, 2, 4, 5) + plane, F32),
            pltpu.VMEM((2, 7) + plane, F32),
            pltpu.VMEM((2, 7) + plane, F32),
            pltpu.VMEM((LEV, 5) + plane, F32),
            pltpu.VMEM((2, GROUPS, 4, 4, SLABS) + plane, BF16),
            pltpu.VMEM((GROUPS, 4, WTAB * CY, 256), BF16),
            pltpu.VMEM((WTAB, 4 * HALF * CY, CX), BF16),
            pltpu.VMEM((2, GROUPS, 4, HALF) + plane, BF16),
            pltpu.VMEM((2, GROUPS, 4, HALF) + plane, BF16),
            pltpu.VMEM((3, LEV) + plane, F32),
            pltpu.SemaphoreType.DMA((LEV,)),
            pltpu.SemaphoreType.DMA((4,)),
            pltpu.SemaphoreType.DMA((4,)),
            pltpu.SemaphoreType.DMA,
            pltpu.SemaphoreType.DMA((2, GROUPS, 14)),
            pltpu.SemaphoreType.DMA((2, GROUPS, 14)),
            pltpu.SemaphoreType.DMA((2,)),
            pltpu.SemaphoreType.DMA((2,)),
            pltpu.SemaphoreType.DMA((2, GROUPS, 4)),
            pltpu.SemaphoreType.DMA((2, GROUPS, 4)),
        ],
        compiler_params=pltpu.CompilerParams(
            collective_id=0, has_side_effects=True, vmem_limit_bytes=60 * 2**20
        ),
        name="interval",
    )(
        state_field[0],
        courant[0],
        diffusivity[0],
        coupling_rate[0],
        weight_table,
        source_row[0],
        destination_tile_ids.reshape(1, ENTRIES),
        dest_row[0],
        weight_slot[0],
    )
    out = pl.pallas_call(
        combine,
        out_shape=jax.ShapeDtypeStruct((LEV, FIELDS) + plane, F32),
        in_specs=[hbm, vmem, vmem],
        out_specs=hbm,
        scratch_shapes=[
            pltpu.VMEM((LEV, FIELDS) + plane, F32),
            pltpu.SemaphoreType.DMA((LEV,)),
            pltpu.SemaphoreType.DMA((LEV,)),
        ],
        compiler_params=pltpu.CompilerParams(vmem_limit_bytes=60 * 2**20),
        name="combine",
    )(solved, gain, incoming)
    return out[None]


def solution(mesh):
    return jax.shard_map(
        per_device,
        mesh=mesh,
        in_specs=(
            P("comp", None, None, None, "tile"),
            P("comp", None, None, None, "tile"),
            P("comp", None, None, "tile"),
            P("comp", None, "tile"),
            P(),
            P("comp", "tile", None),
            P("comp", "tile", None, None),
            P("comp", "tile", None),
            P("comp", "tile", None),
        ),
        out_specs=P("comp", None, None, None, "tile"),
        check_vma=False,
    )
```

```python
import jax
import jax.numpy as jnp
from jax import lax
from jax.experimental import pallas as pl
from jax.experimental.pallas import tpu as pltpu
from jax.sharding import PartitionSpec as P

MESH = pl.DeviceIdType.MESH
NT = (((1,), (1,)), ((), ()))
LEV, FIELDS, CY, CX = 8, 24, 16, 128
ENTRIES, WTAB = 384, 32
GROUPS = 3
GF = FIELDS // GROUPS
SLABS = GF + 1
AXES = ((0, 1, 2), (1, 2, 0), (2, 0, 1))
F32, BF16, I32 = jnp.float32, jnp.bfloat16, jnp.int32


def iota(shape, dim):
    return lax.broadcasted_iota(I32, shape, dim)


def roll_lanes(value, shift):
    return pltpu.roll(value, shift % CX, 1)


def stencil_coefs(cx, cy):
    rows = iota(cx.shape, 0)
    cxp, cxm = jnp.maximum(cx, 0.0), jnp.minimum(cx, 0.0)
    cy = jnp.where(rows < CY - 1, cy, 0.0)
    cyp, cym = jnp.maximum(cy, 0.0), jnp.minimum(cy, 0.0)
    west = roll_lanes(cxp, 1)
    south = pltpu.roll(cyp, 1, 0)
    centre = 1.0 - cxp + roll_lanes(cxm, 1) - cyp + pltpu.roll(cym, 1, 0)
    return centre, -cxm, west, -cym, south


def one_step(a, coefs):
    centre, east, west, north, south = coefs
    return (
        centre * a
        + east * roll_lanes(a, CX - 1)
        + west * roll_lanes(a, 1)
        + north * pltpu.roll(a, CY - 1, 0)
        + south * pltpu.roll(a, 1, 0)
    )


def kernel(
    state_hbm,
    courant_hbm,
    diff_hbm,
    rate_hbm,
    weight_hbm,
    srow_hbm,
    dest_hbm,
    drow_hbm,
    wslot_hbm,
    solved_hbm,
    gain_ref,
    incoming_ref,
    state,
    courant_ref,
    diff_ref,
    rate_ref,
    entries,
    weight,
    packed,
    strips,
    strip_coef,
    halo_out,
    halo_in,
    coef,
    gath,
    pick,
    spread,
    outgoing,
    arrived,
    solve_coef,
    load_sem,
    entry_sem,
    small_sem,
    store_sem,
    ag_send,
    ag_recv,
    halo_send,
    halo_recv,
    sc_send,
    sc_recv,
):
    comp, tile = lax.axis_index("comp"), lax.axis_index("tile")
    coords = (tile >> 4, (tile >> 2) & 3, tile & 3)

    def shifted(axis, step):
        place = 4 - 2 * axis
        here = (tile >> place) & 3
        return tile + ((((here + step) & 3) - here) << place)

    right, left = (tile + 1) & 63, (tile + 63) & 63
    barrier = pltpu.get_barrier_semaphore()
    greeted = [(comp, shifted(axis, step)) for axis in range(3) for step in (1, 2, 3)]
    greeted += [(comp, right), (comp, left), (1 - comp, tile)]
    greeted += [(1 - comp, shifted(axis, step)) for axis in range(3) for step in (1, 2, 3)]
    for target in greeted:
        pl.semaphore_signal(barrier, inc=1, device_id=target, device_id_type=MESH)

    loads = [
        pltpu.make_async_copy(state_hbm.at[k], state.at[k], load_sem.at[k]) for k in range(LEV)
    ]
    entry_loads = [
        pltpu.make_async_copy(source, entries.at[pl.ds(n, 1)], entry_sem.at[n])
        for n, source in enumerate((dest_hbm, srow_hbm, drow_hbm, wslot_hbm))
    ]
    small_loads = [
        pltpu.make_async_copy(source, target, small_sem.at[n])
        for n, (source, target) in enumerate(
            ((courant_hbm, courant_ref), (diff_hbm, diff_ref), (rate_hbm, rate_ref), (weight_hbm, weight))
        )
    ]
    loads[0].start()
    for load in entry_loads:
        load.start()
    small_loads[0].start()
    for load in loads[1:]:
        load.start()
    for load in small_loads[1:]:
        load.start()

    for load in entry_loads:
        load.wait()
    targets, srow, drow, wslot = (entries[n : n + 1] for n in range(4))
    named = (iota((64, ENTRIES), 0) == targets).astype(F32)
    before = (iota((ENTRIES, ENTRIES), 0) < iota((ENTRIES, ENTRIES), 1)).astype(F32)
    counts = jnp.dot(named.astype(BF16), before.astype(BF16), preferred_element_type=F32)
    rank = jnp.sum(named * counts, axis=0, keepdims=True).astype(I32)
    rel = (
        ((targets >> 4) - coords[0]) & 3,
        ((targets >> 2) - coords[1]) & 3,
        (targets - coords[2]) & 3,
    )
    kind, quarter = iota((16, ENTRIES), 0) >> 2, iota((16, ENTRIES), 0) & 3
    values = jnp.where(kind == 0, wslot, jnp.where(kind == 1, srow, drow + 1))
    for g, (u, v, q) in enumerate(AXES):
        spot = (rel[u] * 4 + rel[v]) * 8 + rank
        hot = (iota((CX, ENTRIES), 0) == spot).astype(F32).astype(BF16)
        kept = jnp.where((quarter == rel[q]) & (kind < 3), values, 0)
        table = lax.dot_general(kept.astype(F32).astype(BF16), hot, NT, preferred_element_type=F32)
        gath[g, 0, 0, GF] = table.astype(BF16)

    loads[0].wait()
    for g in range(GROUPS):
        gath[g, 0, 0, :GF] = state[0, g * GF : (g + 1) * GF].astype(BF16)

    pl.semaphore_wait(barrier, len(greeted))

    def remote(src, dst, send, recv, target):
        return pltpu.make_async_remote_copy(
            src_ref=src,
            dst_ref=dst,
            send_sem=send,
            recv_sem=recv,
            device_id=target,
            device_id_type=MESH,
        )

    def gather_copy(g, number):
        u, v = g, (g + 1) % 3
        block = lambda i, j: gath.at[g, i, j]
        step = number % 3 + 1
        there = 4 - step
        others = pl.ds(1, 3)
        src, dst, axis = (
            (block(0, 0), block(0, there), u),
            (block(0, 0), block(there, 0), v),
            (block(0, others), block(there, others), v),
        )[number // 3]
        return remote(
            src, dst, ag_send.at[g, number], ag_recv.at[g, number], (comp, shifted(axis, step))
        )

    for number in (0, 2, 1, 3, 5, 4):
        for g in range(GROUPS):
            gather_copy(g, number).start()

    def pass_on(g):
        for number in range(3):
            gather_copy(g, number).wait_recv()
        for number in (6, 8, 7):
            gather_copy(g, number).start()

    for load in loads[1:]:
        load.wait()
    small_loads[0].wait()
    lanes = iota((CY, CX), 1)
    group_of, place = lanes >> 4, lanes & 15

    def pack_level(k, carry):
        for m in range(3):
            value = roll_lanes(state[k, m * 8], 8)
            for i in range(1, 8):
                value = jnp.where(group_of == i, roll_lanes(state[k, m * 8 + i], 16 * i + 8), value)
            packed[k * 3 + m] = value
        return carry

    lax.fori_loop(0, LEV, pack_level, 0)
    planes = [(c, k) for c in range(2) for k in range(LEV)]
    spare = [jnp.where(lanes < 16, roll_lanes(courant_ref[c, k], 8), 0.0) for c, k in planes]
    for shift in (16, 32, 64):
        spare = [value + roll_lanes(value, shift) for value in spare]
    for e, value in enumerate(spare):
        packed[24 + e] = value
    quad = (lanes >> 2) & 3
    for n in range(10):
        for side, base in ((0, 4), (1, 8)):
            value = roll_lanes(packed[4 * n], -base)
            for t in range(1, 4):
                value = jnp.where(quad == t, roll_lanes(packed[4 * n + t], 4 * t - base), value)
            halo_out[side, n] = value
    halos = [
        remote(halo_out.at[side], halo_in.at[side], halo_send.at[side], halo_recv.at[side], (comp, target))
        for side, target in ((0, right), (1, left))
    ]
    for copy in halos:
        copy.start()

    def level_coefs(k, carry):
        for n, value in enumerate(stencil_coefs(courant_ref[0, k], courant_ref[1, k])):
            coef[k, n] = value
        return carry

    for k in range(LEV):
        level_coefs(k, 0)

    def transport_step(n, carry):
        k = n >> 2
        coefs = [coef[k, i] for i in range(5)]
        for f in range(FIELDS):
            state[k, f] = one_step(state[k, f], coefs)
        return carry

    def transport_level(k):
        coefs = [coef[k, i] for i in range(5)]
        for step in range(4):
            for f in range(FIELDS):
                state[k, f] = one_step(state[k, f], coefs)

    for g in range(GROUPS):
        pass_on(g)

    for copy in halos:
        copy.wait_recv()
    mid = (place >= 8) & (place < 12)

    def strip(side, p):
        n, t = p >> 2, p & 3
        if side == 0:
            return jnp.where(place < 4, roll_lanes(halo_in[0, n], -4 * t), roll_lanes(packed[p], -4))
        return jnp.where(mid, roll_lanes(halo_in[1, n], 8 - 4 * t), packed[p])

    for p in range(3 * LEV):
        for side in range(2):
            strips[side, p // 12, p % 12] = strip(side, p)
    for k in range(LEV):
        for side in range(2):
            values = stencil_coefs(strip(side, 24 + k), strip(side, 32 + k))
            for n, value in enumerate(values):
                strip_coef[side, k >> 2, k & 3, n] = value

    def strip_step(n, carry):
        half = n >> 2
        for j in range(4):
            for side in range(2):
                coefs = [strip_coef[side, half, j, i] for i in range(5)]
                for m in range(3):
                    p = j * 3 + m
                    strips[side, half, p] = one_step(strips[side, half, p], coefs)
        return carry

    lax.fori_loop(0, 8, strip_step, 0)
    for p in range(3 * LEV):
        i, r = p // 12, p % 12
        packed[p] = jnp.where(place < 4, roll_lanes(strips[1, i, r], -4), strips[0, i, r])

    lax.fori_loop(12, 32, transport_step, 0)

    small_loads[3].wait()
    rows_p, rows_q = iota((WTAB * CY, CX), 0), iota((256, CX), 0)
    lane_p = iota((1, CX), 1) >> 3

    def scatter_copy(g, d):
        target = (1 - comp, tile if d == 0 else shifted((g + 2) % 3, d))
        return remote(
            outgoing.at[g, d], arrived.at[g, (4 - d) % 4], sc_send.at[g, d], sc_recv.at[g, d], target
        )

    def remap(g, carry):
        for number in range(3, 9):
            gather_copy(g, number).wait_recv()
        table = jnp.zeros((CY, CX), F32)
        for p in range(16):
            rv, ru = p // 4, p % 4
            offset = ((-ru % 4) * 4 + (-rv % 4)) * 8
            moved = roll_lanes(gath[g, rv, ru, GF].astype(F32), p * 8 - offset)
            table = jnp.where((lanes >> 3) == p, moved, table)
        codes = table.astype(I32)
        for d in range(4):
            w_e, r_e, y_e = codes[d : d + 1], codes[4 + d : 5 + d], codes[8 + d : 9 + d]
            into = (rows_p == jnp.where(y_e > 0, w_e * CY + y_e - 1, -1)).astype(F32).astype(BF16)
            outof = (rows_q == lane_p * CY + r_e).astype(F32).astype(BF16)
            pick[d] = lax.dot_general(into, outof, NT, preferred_element_type=F32).astype(BF16)
        for d in range(4):
            for pair in range(GF // 2):
                blocks = jnp.concatenate(
                    [gath[g, :, :, 2 * pair + i].reshape(256, CX) for i in range(2)], axis=1
                )
                summed = jnp.dot(pick[d], blocks, preferred_element_type=F32).astype(BF16)
                for i in range(2):
                    for w in range(WTAB):
                        row = (d * GF + 2 * pair + i) * CY
                        spread[w, row : row + CY] = summed[w * CY : (w + 1) * CY, i * CX : (i + 1) * CX]
        transport_level(g)
        table_all = jnp.concatenate([weight[w] for w in range(WTAB)], axis=1)
        rows = GF * CY
        for d in range(0, 4, 2):
            chosen = jnp.concatenate([spread[w, d * rows : (d + 2) * rows] for w in range(WTAB)], axis=1)
            result = lax.dot_general(chosen, table_all, NT, preferred_element_type=F32).astype(BF16)
            for i in range(2):
                outgoing[g, d + i] = result[i * rows : (i + 1) * rows].reshape(GF, CY, CX)
        for d in range(4):
            scatter_copy(g, d).start()
        return carry

    lax.fori_loop(0, GROUPS, remap, 0)

    small_loads[1].wait()
    small_loads[2].wait()
    ratio = jnp.zeros((CY, CX), F32)
    gain = None
    gains, ratios = [], []
    for k in range(LEV):
        above = diff_ref[k] if k < LEV - 1 else jnp.zeros((CY, CX), F32)
        below = diff_ref[k - 1] if k > 0 else jnp.zeros((CY, CX), F32)
        inverse = 1.0 / (1.0 + below + above - below * ratio)
        ratio = above * inverse
        solve_coef[0, k] = inverse
        solve_coef[1, k] = below * inverse
        solve_coef[2, k] = ratio
        gain = inverse if k == 0 else below * inverse * gain
        gains.append(gain)
        ratios.append(ratio)
    value = jnp.zeros((CY, CX), F32)
    for k in reversed(range(LEV)):
        value = gains[k] + ratios[k] * value
        gain_ref[k] = value * rate_ref[...]

    edge = (lanes < 4) | (lanes >= CX - 4)

    def solve_fields(n, carry):
        m = n >> 1
        for j in range(4):
            f = n * 4 + j
            turn = CX - 4 - 16 * ((n & 1) * 4 + j)
            solved = jnp.zeros((CY, CX), F32)
            kept = []
            for k in range(LEV):
                value = jnp.where(edge, pltpu.roll(packed[k * 3 + m], turn, 1), state[k, f])
                solved = solve_coef[0, k] * value + solve_coef[1, k] * solved
                kept.append(solved)
            upper = kept[-1]
            state[LEV - 1, f] = upper
            for k in reversed(range(LEV - 1)):
                upper = kept[k] + solve_coef[2, k] * upper
                state[k, f] = upper
        return carry

    lax.fori_loop(0, FIELDS // 4, solve_fields, 0)
    store = pltpu.make_async_copy(state, solved_hbm, store_sem)
    store.start()

    for g in range(GROUPS):
        for d in range(4):
            scatter_copy(g, d).wait_recv()
        total = arrived[g, 0].astype(F32)
        for d in range(1, 4):
            total = total + arrived[g, d].astype(F32)
        incoming_ref[g * GF : (g + 1) * GF] = total

    def finish(g, carry):
        for number in range(9):
            gather_copy(g, number).wait_send()
        for d in range(4):
            scatter_copy(g, d).wait_send()
        return carry

    lax.fori_loop(0, GROUPS, finish, 0)
    for copy in halos:
        copy.wait_send()
    store.wait()


def combine(solved_hbm, gain_ref, incoming_ref, out_hbm, held, load_sem, store_sem):
    loads = [pltpu.make_async_copy(solved_hbm.at[k], held.at[k], load_sem.at[k]) for k in range(LEV)]
    stores = [pltpu.make_async_copy(held.at[k], out_hbm.at[k], store_sem.at[k]) for k in range(LEV)]
    for load in loads:
        load.start()
    for k in range(LEV):
        loads[k].wait()
        gain = gain_ref[k]
        for f in range(FIELDS):
            held[k, f] = held[k, f] + gain * incoming_ref[f]
        stores[k].start()
    for store in stores:
        store.wait()


def per_device(
    state_field,
    courant,
    diffusivity,
    coupling_rate,
    weight_table,
    source_row,
    destination_tile_ids,
    dest_row,
    weight_slot,
):
    vmem, hbm = pl.BlockSpec(memory_space=pltpu.VMEM), pl.BlockSpec(memory_space=pltpu.HBM)
    plane = (CY, CX)
    solved, gain, incoming = pl.pallas_call(
        kernel,
        out_shape=(
            jax.ShapeDtypeStruct((LEV, FIELDS) + plane, F32),
            jax.ShapeDtypeStruct((LEV,) + plane, F32),
            jax.ShapeDtypeStruct((FIELDS,) + plane, F32),
        ),
        in_specs=[hbm] * 9,
        out_specs=(hbm, vmem, vmem),
        scratch_shapes=[
            pltpu.VMEM((LEV, FIELDS) + plane, F32),
            pltpu.VMEM((2, LEV) + plane, F32),
            pltpu.VMEM((LEV,) + plane, F32),
            pltpu.VMEM(plane, F32),
            pltpu.VMEM((4, ENTRIES), I32),
            pltpu.VMEM((WTAB, CX, CX), BF16),
            pltpu.VMEM((40,) + plane, F32),
            pltpu.VMEM((2, 2, 12) + plane, F32),
            pltpu.VMEM((2, 2, 4, 5) + plane, F32),
            pltpu.VMEM((2, 10) + plane, F32),
            pltpu.VMEM((2, 10) + plane, F32),
            pltpu.VMEM((LEV, 5) + plane, F32),
            pltpu.VMEM((GROUPS, 4, 4, SLABS) + plane, BF16),
            pltpu.VMEM((4, WTAB * CY, 256), BF16),
            pltpu.VMEM((WTAB, 4 * GF * CY, CX), BF16),
            pltpu.VMEM((GROUPS, 4, GF) + plane, BF16),
            pltpu.VMEM((GROUPS, 4, GF) + plane, BF16),
            pltpu.VMEM((3, LEV) + plane, F32),
            pltpu.SemaphoreType.DMA((LEV,)),
            pltpu.SemaphoreType.DMA((4,)),
            pltpu.SemaphoreType.DMA((4,)),
            pltpu.SemaphoreType.DMA,
            pltpu.SemaphoreType.DMA((GROUPS, 9)),
            pltpu.SemaphoreType.DMA((GROUPS, 9)),
            pltpu.SemaphoreType.DMA((2,)),
            pltpu.SemaphoreType.DMA((2,)),
            pltpu.SemaphoreType.DMA((GROUPS, 4)),
            pltpu.SemaphoreType.DMA((GROUPS, 4)),
        ],
        compiler_params=pltpu.CompilerParams(
            collective_id=0, has_side_effects=True, vmem_limit_bytes=60 * 2**20
        ),
        name="interval",
    )(
        state_field[0],
        courant[0],
        diffusivity[0],
        coupling_rate[0],
        weight_table,
        source_row[0],
        destination_tile_ids.reshape(1, ENTRIES),
        dest_row[0],
        weight_slot[0],
    )
    out = pl.pallas_call(
        combine,
        out_shape=jax.ShapeDtypeStruct((LEV, FIELDS) + plane, F32),
        in_specs=[hbm, vmem, vmem],
        out_specs=hbm,
        scratch_shapes=[
            pltpu.VMEM((LEV, FIELDS) + plane, F32),
            pltpu.SemaphoreType.DMA((LEV,)),
            pltpu.SemaphoreType.DMA((LEV,)),
        ],
        compiler_params=pltpu.CompilerParams(vmem_limit_bytes=60 * 2**20),
        name="combine",
    )(solved, gain, incoming)
    return out[None]


def solution(mesh):
    return jax.shard_map(
        per_device,
        mesh=mesh,
        in_specs=(
            P("comp", None, None, None, "tile"),
            P("comp", None, None, None, "tile"),
            P("comp", None, None, "tile"),
            P("comp", None, "tile"),
            P(),
            P("comp", "tile", None),
            P("comp", "tile", None, None),
            P("comp", "tile", None),
            P("comp", "tile", None),
        ),
        out_specs=P("comp", None, None, None, "tile"),
        check_vma=False,
    )
```

```python
import jax
import jax.numpy as jnp
from jax import lax
from jax.experimental import pallas as pl
from jax.experimental.pallas import tpu as pltpu
from jax.sharding import PartitionSpec as P

MESH = pl.DeviceIdType.MESH
NT = (((1,), (1,)), ((), ()))
LEV, FIELDS, CY, CX = 8, 24, 16, 128
ENTRIES, WTAB = 384, 32
GROUPS = 3
GF = FIELDS // GROUPS
HALF = GF // 2
SLABS = GF + 1
CUT = HALF + 1
AXES = ((0, 1, 2), (1, 2, 0), (2, 0, 1))
F32, BF16, I32 = jnp.float32, jnp.bfloat16, jnp.int32


def iota(shape, dim):
    return lax.broadcasted_iota(I32, shape, dim)


def roll_lanes(value, shift):
    return pltpu.roll(value, shift % CX, 1)


def stencil_coefs(cx, cy):
    rows = iota(cx.shape, 0)
    cxp, cxm = jnp.maximum(cx, 0.0), jnp.minimum(cx, 0.0)
    cy = jnp.where(rows < CY - 1, cy, 0.0)
    cyp, cym = jnp.maximum(cy, 0.0), jnp.minimum(cy, 0.0)
    west = roll_lanes(cxp, 1)
    south = pltpu.roll(cyp, 1, 0)
    centre = 1.0 - cxp + roll_lanes(cxm, 1) - cyp + pltpu.roll(cym, 1, 0)
    return centre, -cxm, west, -cym, south


def one_step(a, coefs):
    centre, east, west, north, south = coefs
    return (
        centre * a
        + east * roll_lanes(a, CX - 1)
        + west * roll_lanes(a, 1)
        + north * pltpu.roll(a, CY - 1, 0)
        + south * pltpu.roll(a, 1, 0)
    )


def kernel(
    state_hbm,
    courant_hbm,
    diff_hbm,
    rate_hbm,
    weight_hbm,
    srow_hbm,
    dest_hbm,
    drow_hbm,
    wslot_hbm,
    state,
    gain_ref,
    incoming_ref,
    courant_ref,
    diff_ref,
    rate_ref,
    entries,
    weight,
    packed,
    strips,
    strip_coef,
    halo_out,
    halo_in,
    coef,
    gath,
    pick,
    spread,
    outgoing,
    arrived,
    solve_coef,
    load_sem,
    entry_sem,
    small_sem,
    ag_send,
    ag_recv,
    halo_send,
    halo_recv,
    sc_send,
    sc_recv,
):
    comp, tile = lax.axis_index("comp"), lax.axis_index("tile")
    coords = (tile >> 4, (tile >> 2) & 3, tile & 3)

    def shifted(axis, step):
        place = 4 - 2 * axis
        here = (tile >> place) & 3
        return tile + ((((here + step) & 3) - here) << place)

    right, left = (tile + 1) & 63, (tile + 63) & 63
    barrier = pltpu.get_barrier_semaphore()
    greeted = [(comp, shifted(axis, step)) for axis in range(3) for step in (1, 2, 3)]
    greeted += [(comp, right), (comp, left), (1 - comp, tile)]
    greeted += [(1 - comp, shifted(axis, step)) for axis in range(3) for step in (1, 2, 3)]
    for target in greeted:
        pl.semaphore_signal(barrier, inc=1, device_id=target, device_id_type=MESH)

    loads = [
        pltpu.make_async_copy(state_hbm.at[k], state.at[k], load_sem.at[k]) for k in range(LEV)
    ]
    entry_loads = [
        pltpu.make_async_copy(source, entries.at[pl.ds(n, 1)], entry_sem.at[n])
        for n, source in enumerate((dest_hbm, srow_hbm, drow_hbm, wslot_hbm))
    ]
    small_loads = [
        pltpu.make_async_copy(source, target, small_sem.at[n])
        for n, (source, target) in enumerate(
            ((courant_hbm, courant_ref), (diff_hbm, diff_ref), (rate_hbm, rate_ref), (weight_hbm, weight))
        )
    ]
    loads[0].start()
    for load in entry_loads:
        load.start()
    small_loads[0].start()
    for load in loads[1:]:
        load.start()
    for load in small_loads[1:]:
        load.start()

    for load in entry_loads:
        load.wait()
    targets, srow, drow, wslot = (entries[n : n + 1] for n in range(4))
    named = (iota((64, ENTRIES), 0) == targets).astype(F32)
    before = (iota((ENTRIES, ENTRIES), 0) < iota((ENTRIES, ENTRIES), 1)).astype(F32)
    counts = jnp.dot(named.astype(BF16), before.astype(BF16), preferred_element_type=F32)
    rank = jnp.sum(named * counts, axis=0, keepdims=True).astype(I32)
    rel = (
        ((targets >> 4) - coords[0]) & 3,
        ((targets >> 2) - coords[1]) & 3,
        (targets - coords[2]) & 3,
    )
    kind, quarter = iota((16, ENTRIES), 0) >> 2, iota((16, ENTRIES), 0) & 3
    values = jnp.where(kind == 0, wslot, jnp.where(kind == 1, srow, drow + 1))
    for g, (u, v, q) in enumerate(AXES):
        spot = (rel[u] * 4 + rel[v]) * 8 + rank
        hot = (iota((CX, ENTRIES), 0) == spot).astype(F32).astype(BF16)
        kept = jnp.where((quarter == rel[q]) & (kind < 3), values, 0)
        table = lax.dot_general(kept.astype(F32).astype(BF16), hot, NT, preferred_element_type=F32)
        gath[g, 0, 0, 0] = table.astype(BF16)

    loads[0].wait()
    for g in range(GROUPS):
        gath[g, 0, 0, 1:] = state[0, g * GF : (g + 1) * GF].astype(BF16)

    pl.semaphore_wait(barrier, len(greeted))

    def remote(src, dst, send, recv, target):
        return pltpu.make_async_remote_copy(
            src_ref=src,
            dst_ref=dst,
            send_sem=send,
            recv_sem=recv,
            device_id=target,
            device_id_type=MESH,
        )

    parts = (pl.ds(0, CUT), pl.ds(CUT, SLABS - CUT))

    def gather_copy(g, number):
        u, v = g, (g + 1) % 3
        step = number % 3 + 1
        there = 4 - step
        others = pl.ds(1, 3)
        src, dst, axis = (
            (gath.at[g, 0, 0], gath.at[g, 0, there], u),
            (gath.at[g, 0, 0, parts[0]], gath.at[g, there, 0, parts[0]], v),
            (gath.at[g, 0, others, parts[0]], gath.at[g, there, others, parts[0]], v),
            (gath.at[g, 0, :, parts[1]], gath.at[g, there, :, parts[1]], v),
        )[number // 3]
        return remote(
            src, dst, ag_send.at[g, number], ag_recv.at[g, number], (comp, shifted(axis, step))
        )

    for number in (0, 2, 1, 3, 5, 4):
        for g in range(GROUPS):
            gather_copy(g, number).start()

    def pass_on(g):
        for number in range(3):
            gather_copy(g, number).wait_recv()
        for number in (6, 8, 7):
            gather_copy(g, number).start()

    for load in loads[1:]:
        load.wait()
    small_loads[0].wait()
    lanes = iota((CY, CX), 1)
    group_of, place = lanes >> 4, lanes & 15

    def pack_level(k, carry):
        for m in range(3):
            value = roll_lanes(state[k, m * 8], 8)
            for i in range(1, 8):
                value = jnp.where(group_of == i, roll_lanes(state[k, m * 8 + i], 16 * i + 8), value)
            packed[k * 3 + m] = value
        return carry

    lax.fori_loop(0, LEV, pack_level, 0)
    planes = [(c, k) for c in range(2) for k in range(LEV)]
    spare = [jnp.where(lanes < 16, roll_lanes(courant_ref[c, k], 8), 0.0) for c, k in planes]
    for shift in (16, 32, 64):
        spare = [value + roll_lanes(value, shift) for value in spare]
    for e, value in enumerate(spare):
        packed[24 + e] = value
    quad = (lanes >> 2) & 3
    for n in range(10):
        for side, base in ((0, 4), (1, 8)):
            value = roll_lanes(packed[4 * n], -base)
            for t in range(1, 4):
                value = jnp.where(quad == t, roll_lanes(packed[4 * n + t], 4 * t - base), value)
            halo_out[side, n] = value
    halos = [
        remote(halo_out.at[side], halo_in.at[side], halo_send.at[side], halo_recv.at[side], (comp, target))
        for side, target in ((0, right), (1, left))
    ]
    for copy in halos:
        copy.start()

    def level_coefs(k, carry):
        for n, value in enumerate(stencil_coefs(courant_ref[0, k], courant_ref[1, k])):
            coef[k, n] = value
        return carry

    for k in range(LEV):
        level_coefs(k, 0)

    def transport_step(n, carry):
        k = n >> 2
        coefs = [coef[k, i] for i in range(5)]
        for f in range(FIELDS):
            state[k, f] = one_step(state[k, f], coefs)
        return carry

    def transport_level(k):
        coefs = [coef[k, i] for i in range(5)]
        for step in range(4):
            for f in range(FIELDS):
                state[k, f] = one_step(state[k, f], coefs)

    for g in range(GROUPS):
        pass_on(g)

    for copy in halos:
        copy.wait_recv()
    mid = (place >= 8) & (place < 12)

    def strip(side, p):
        n, t = p >> 2, p & 3
        if side == 0:
            return jnp.where(place < 4, roll_lanes(halo_in[0, n], -4 * t), roll_lanes(packed[p], -4))
        return jnp.where(mid, roll_lanes(halo_in[1, n], 8 - 4 * t), packed[p])

    for p in range(3 * LEV):
        for side in range(2):
            strips[side, p // 12, p % 12] = strip(side, p)
    for k in range(LEV):
        for side in range(2):
            values = stencil_coefs(strip(side, 24 + k), strip(side, 32 + k))
            for n, value in enumerate(values):
                strip_coef[side, k >> 2, k & 3, n] = value

    for number in (9, 11, 10):
        for g in range(GROUPS):
            gather_copy(g, number).start()

    def strip_step(n, carry):
        half = n >> 2
        for j in range(4):
            for side in range(2):
                coefs = [strip_coef[side, half, j, i] for i in range(5)]
                for m in range(3):
                    p = j * 3 + m
                    strips[side, half, p] = one_step(strips[side, half, p], coefs)
        return carry

    lax.fori_loop(0, 8, strip_step, 0)
    for p in range(3 * LEV):
        i, r = p // 12, p % 12
        packed[p] = jnp.where(place < 4, roll_lanes(strips[1, i, r], -4), strips[0, i, r])

    lax.fori_loop(24, 32, transport_step, 0)

    small_loads[3].wait()
    rows_p, rows_q = iota((WTAB * CY, CX), 0), iota((256, CX), 0)
    lane_p = iota((1, CX), 1) >> 3

    def scatter_copy(part, g, d):
        target = (1 - comp, tile if d == 0 else shifted((g + 2) % 3, d))
        return remote(
            outgoing.at[part, g, d],
            arrived.at[part, g, (4 - d) % 4],
            sc_send.at[part, g, d],
            sc_recv.at[part, g, d],
            target,
        )

    def remap(part, g, carry):
        for number in range(3, 9) if part == 0 else range(9, 12):
            gather_copy(g, number).wait_recv()
        if part == 0:
            table = jnp.zeros((CY, CX), F32)
            for p in range(16):
                rv, ru = p // 4, p % 4
                offset = ((-ru % 4) * 4 + (-rv % 4)) * 8
                moved = roll_lanes(gath[g, rv, ru, 0].astype(F32), p * 8 - offset)
                table = jnp.where((lanes >> 3) == p, moved, table)
            codes = table.astype(I32)
            for d in range(4):
                w_e, r_e, y_e = codes[d : d + 1], codes[4 + d : 5 + d], codes[8 + d : 9 + d]
                into = (rows_p == jnp.where(y_e > 0, w_e * CY + y_e - 1, -1)).astype(F32).astype(BF16)
                outof = (rows_q == lane_p * CY + r_e).astype(F32).astype(BF16)
                pick[g, d] = lax.dot_general(into, outof, NT, preferred_element_type=F32).astype(BF16)
        first = 1 + part * HALF
        for d in range(4):
            for pair in range(HALF // 2):
                blocks = jnp.concatenate(
                    [gath[g, :, :, first + 2 * pair + i].reshape(256, CX) for i in range(2)], axis=1
                )
                summed = jnp.dot(pick[g, d], blocks, preferred_element_type=F32).astype(BF16)
                for i in range(2):
                    for w in range(WTAB):
                        row = (d * HALF + 2 * pair + i) * CY
                        spread[w, row : row + CY] = summed[w * CY : (w + 1) * CY, i * CX : (i + 1) * CX]
        transport_level(3 * part + g)
        table_all = jnp.concatenate([weight[w] for w in range(WTAB)], axis=1)
        rows = HALF * CY
        for d in range(0, 4, 2):
            chosen = jnp.concatenate([spread[w, d * rows : (d + 2) * rows] for w in range(WTAB)], axis=1)
            result = lax.dot_general(chosen, table_all, NT, preferred_element_type=F32).astype(BF16)
            for i in range(2):
                outgoing[part, g, d + i] = result[i * rows : (i + 1) * rows].reshape(HALF, CY, CX)
        for d in range(4):
            scatter_copy(part, g, d).start()
        return carry

    for part in range(2):
        lax.fori_loop(0, GROUPS, lambda g, carry, part=part: remap(part, g, carry), 0)

    small_loads[1].wait()
    small_loads[2].wait()
    ratio = jnp.zeros((CY, CX), F32)
    gain = None
    gains, ratios = [], []
    for k in range(LEV):
        above = diff_ref[k] if k < LEV - 1 else jnp.zeros((CY, CX), F32)
        below = diff_ref[k - 1] if k > 0 else jnp.zeros((CY, CX), F32)
        inverse = 1.0 / (1.0 + below + above - below * ratio)
        ratio = above * inverse
        solve_coef[0, k] = inverse
        solve_coef[1, k] = below * inverse
        solve_coef[2, k] = ratio
        gain = inverse if k == 0 else below * inverse * gain
        gains.append(gain)
        ratios.append(ratio)
    value = jnp.zeros((CY, CX), F32)
    for k in reversed(range(LEV)):
        value = gains[k] + ratios[k] * value
        gain_ref[k] = value * rate_ref[...]

    edge = (lanes < 4) | (lanes >= CX - 4)

    def solve_fields(n, carry):
        m = n >> 1
        for j in range(4):
            f = n * 4 + j
            turn = CX - 4 - 16 * ((n & 1) * 4 + j)
            solved = jnp.zeros((CY, CX), F32)
            kept = []
            for k in range(LEV):
                value = jnp.where(edge, pltpu.roll(packed[k * 3 + m], turn, 1), state[k, f])
                solved = solve_coef[0, k] * value + solve_coef[1, k] * solved
                kept.append(solved)
            upper = kept[-1]
            state[LEV - 1, f] = upper
            for k in reversed(range(LEV - 1)):
                upper = kept[k] + solve_coef[2, k] * upper
                state[k, f] = upper
        return carry

    lax.fori_loop(0, FIELDS // 4, solve_fields, 0)

    for part in range(2):
        for g in range(GROUPS):
            for d in range(4):
                scatter_copy(part, g, d).wait_recv()
            total = arrived[part, g, 0].astype(F32)
            for d in range(1, 4):
                total = total + arrived[part, g, d].astype(F32)
            start = (2 * g + part) * HALF
            incoming_ref[start : start + HALF] = total

    def finish(g, carry):
        for number in range(12):
            gather_copy(g, number).wait_send()
        for part in range(2):
            for d in range(4):
                scatter_copy(part, g, d).wait_send()
        return carry

    lax.fori_loop(0, GROUPS, finish, 0)
    for copy in halos:
        copy.wait_send()


def per_device(
    state_field,
    courant,
    diffusivity,
    coupling_rate,
    weight_table,
    source_row,
    destination_tile_ids,
    dest_row,
    weight_slot,
):
    vmem, hbm = pl.BlockSpec(memory_space=pltpu.VMEM), pl.BlockSpec(memory_space=pltpu.HBM)
    plane = (CY, CX)
    solved, gain, incoming = pl.pallas_call(
        kernel,
        out_shape=(
            pltpu.VMEM((LEV, FIELDS) + plane, F32),
            pltpu.VMEM((LEV,) + plane, F32),
            pltpu.VMEM((FIELDS,) + plane, F32),
        ),
        in_specs=[hbm] * 9,
        out_specs=(vmem, vmem, vmem),
        scratch_shapes=[
            pltpu.VMEM((2, LEV) + plane, F32),
            pltpu.VMEM((LEV,) + plane, F32),
            pltpu.VMEM(plane, F32),
            pltpu.VMEM((4, ENTRIES), I32),
            pltpu.VMEM((WTAB, CX, CX), BF16),
            pltpu.VMEM((40,) + plane, F32),
            pltpu.VMEM((2, 2, 12) + plane, F32),
            pltpu.VMEM((2, 2, 4, 5) + plane, F32),
            pltpu.VMEM((2, 10) + plane, F32),
            pltpu.VMEM((2, 10) + plane, F32),
            pltpu.VMEM((LEV, 5) + plane, F32),
            pltpu.VMEM((GROUPS, 4, 4, SLABS) + plane, BF16),
            pltpu.VMEM((GROUPS, 4, WTAB * CY, 256), BF16),
            pltpu.VMEM((WTAB, 4 * HALF * CY, CX), BF16),
            pltpu.VMEM((2, GROUPS, 4, HALF) + plane, BF16),
            pltpu.VMEM((2, GROUPS, 4, HALF) + plane, BF16),
            pltpu.VMEM((3, LEV) + plane, F32),
            pltpu.SemaphoreType.DMA((LEV,)),
            pltpu.SemaphoreType.DMA((4,)),
            pltpu.SemaphoreType.DMA((4,)),
            pltpu.SemaphoreType.DMA((GROUPS, 12)),
            pltpu.SemaphoreType.DMA((GROUPS, 12)),
            pltpu.SemaphoreType.DMA((2,)),
            pltpu.SemaphoreType.DMA((2,)),
            pltpu.SemaphoreType.DMA((2, GROUPS, 4)),
            pltpu.SemaphoreType.DMA((2, GROUPS, 4)),
        ],
        compiler_params=pltpu.CompilerParams(
            collective_id=0, has_side_effects=True, vmem_limit_bytes=60 * 2**20
        ),
        name="interval",
    )(
        state_field[0],
        courant[0],
        diffusivity[0],
        coupling_rate[0],
        weight_table,
        source_row[0],
        destination_tile_ids.reshape(1, ENTRIES),
        dest_row[0],
        weight_slot[0],
    )
    return (solved + gain[:, None] * incoming[None])[None]


def solution(mesh):
    return jax.shard_map(
        per_device,
        mesh=mesh,
        in_specs=(
            P("comp", None, None, None, "tile"),
            P("comp", None, None, None, "tile"),
            P("comp", None, None, "tile"),
            P("comp", None, "tile"),
            P(),
            P("comp", "tile", None),
            P("comp", "tile", None, None),
            P("comp", "tile", None),
            P("comp", "tile", None),
        ),
        out_specs=P("comp", None, None, None, "tile"),
        check_vma=False,
    )
```

```python
import jax
import jax.numpy as jnp
from jax import lax
from jax.experimental import pallas as pl
from jax.experimental.pallas import tpu as pltpu
from jax.sharding import PartitionSpec as P

MESH = pl.DeviceIdType.MESH
NT = (((1,), (1,)), ((), ()))
LEV, FIELDS, CY, CX = 8, 24, 16, 128
ENTRIES, WTAB = 384, 32
GROUPS = 3
GF = FIELDS // GROUPS
HALF = GF // 2
SLABS = GF + 1
CUT = HALF + 1
AXES = ((0, 1, 2), (1, 2, 0), (2, 0, 1))
F32, BF16, I32 = jnp.float32, jnp.bfloat16, jnp.int32


def iota(shape, dim):
    return lax.broadcasted_iota(I32, shape, dim)


def roll_lanes(value, shift):
    return pltpu.roll(value, shift % CX, 1)


def stencil_coefs(cx, cy):
    rows = iota(cx.shape, 0)
    cxp, cxm = jnp.maximum(cx, 0.0), jnp.minimum(cx, 0.0)
    cy = jnp.where(rows < CY - 1, cy, 0.0)
    cyp, cym = jnp.maximum(cy, 0.0), jnp.minimum(cy, 0.0)
    west = roll_lanes(cxp, 1)
    south = pltpu.roll(cyp, 1, 0)
    centre = 1.0 - cxp + roll_lanes(cxm, 1) - cyp + pltpu.roll(cym, 1, 0)
    return centre, -cxm, west, -cym, south


def one_step(a, coefs):
    centre, east, west, north, south = coefs
    return (
        centre * a
        + east * roll_lanes(a, CX - 1)
        + west * roll_lanes(a, 1)
        + north * pltpu.roll(a, CY - 1, 0)
        + south * pltpu.roll(a, 1, 0)
    )


def kernel(
    state_hbm,
    courant_hbm,
    diff_hbm,
    rate_hbm,
    weight_hbm,
    srow_hbm,
    dest_hbm,
    drow_hbm,
    wslot_hbm,
    state,
    gain_ref,
    incoming_ref,
    courant_ref,
    diff_ref,
    rate_ref,
    entries,
    weight,
    packed,
    strips,
    strip_coef,
    halo_out,
    halo_in,
    coef,
    gath,
    pick,
    spread,
    outgoing,
    arrived,
    solve_coef,
    load_sem,
    entry_sem,
    small_sem,
    ag_send,
    ag_recv,
    halo_send,
    halo_recv,
    sc_send,
    sc_recv,
):
    comp, tile = lax.axis_index("comp"), lax.axis_index("tile")
    coords = (tile >> 4, (tile >> 2) & 3, tile & 3)

    def shifted(axis, step):
        place = 4 - 2 * axis
        here = (tile >> place) & 3
        return tile + ((((here + step) & 3) - here) << place)

    right, left = (tile + 1) & 63, (tile + 63) & 63
    barrier = pltpu.get_barrier_semaphore()
    greeted = [(comp, shifted(axis, step)) for axis in range(3) for step in (1, 2, 3)]
    greeted += [(comp, right), (comp, left), (1 - comp, tile)]
    greeted += [(1 - comp, shifted(axis, step)) for axis in range(3) for step in (1, 2, 3)]
    for target in greeted:
        pl.semaphore_signal(barrier, inc=1, device_id=target, device_id_type=MESH)

    loads = [
        pltpu.make_async_copy(state_hbm.at[k], state.at[k], load_sem.at[k]) for k in range(LEV)
    ]
    entry_loads = [
        pltpu.make_async_copy(source, entries.at[pl.ds(n, 1)], entry_sem.at[n])
        for n, source in enumerate((dest_hbm, srow_hbm, drow_hbm, wslot_hbm))
    ]
    small_loads = [
        pltpu.make_async_copy(source, target, small_sem.at[n])
        for n, (source, target) in enumerate(
            ((courant_hbm, courant_ref), (diff_hbm, diff_ref), (rate_hbm, rate_ref), (weight_hbm, weight))
        )
    ]
    loads[0].start()
    for load in entry_loads:
        load.start()
    small_loads[0].start()
    for load in loads[1:]:
        load.start()
    for load in small_loads[1:]:
        load.start()

    for load in entry_loads:
        load.wait()
    targets, srow, drow, wslot = (entries[n : n + 1] for n in range(4))
    named = (iota((64, ENTRIES), 0) == targets).astype(F32)
    before = (iota((ENTRIES, ENTRIES), 0) < iota((ENTRIES, ENTRIES), 1)).astype(F32)
    counts = jnp.dot(named.astype(BF16), before.astype(BF16), preferred_element_type=F32)
    rank = jnp.sum(named * counts, axis=0, keepdims=True).astype(I32)
    rel = (
        ((targets >> 4) - coords[0]) & 3,
        ((targets >> 2) - coords[1]) & 3,
        (targets - coords[2]) & 3,
    )
    kind, quarter = iota((16, ENTRIES), 0) >> 2, iota((16, ENTRIES), 0) & 3
    values = jnp.where(kind == 0, wslot, jnp.where(kind == 1, srow, drow + 1))
    for g, (u, v, q) in enumerate(AXES):
        spot = (rel[u] * 4 + rel[v]) * 8 + rank
        hot = (iota((CX, ENTRIES), 0) == spot).astype(F32).astype(BF16)
        kept = jnp.where((quarter == rel[q]) & (kind < 3), values, 0)
        table = lax.dot_general(kept.astype(F32).astype(BF16), hot, NT, preferred_element_type=F32)
        gath[g, 0, 0, 0] = table.astype(BF16)

    loads[0].wait()
    for g in range(GROUPS):
        gath[g, 0, 0, 1:] = state[0, g * GF : (g + 1) * GF].astype(BF16)

    pl.semaphore_wait(barrier, len(greeted))

    def remote(src, dst, send, recv, target):
        return pltpu.make_async_remote_copy(
            src_ref=src,
            dst_ref=dst,
            send_sem=send,
            recv_sem=recv,
            device_id=target,
            device_id_type=MESH,
        )

    parts = (pl.ds(0, CUT), pl.ds(CUT, SLABS - CUT))

    def gather_copy(g, number):
        u, v = g, (g + 1) % 3
        step = number % 3 + 1
        there = 4 - step
        others = pl.ds(1, 3)
        src, dst, axis = (
            (gath.at[g, 0, 0], gath.at[g, 0, there], u),
            (gath.at[g, 0, 0, parts[0]], gath.at[g, there, 0, parts[0]], v),
            (gath.at[g, 0, others, parts[0]], gath.at[g, there, others, parts[0]], v),
            (gath.at[g, 0, :, parts[1]], gath.at[g, there, :, parts[1]], v),
        )[number // 3]
        return remote(
            src, dst, ag_send.at[g, number], ag_recv.at[g, number], (comp, shifted(axis, step))
        )

    for number in (0, 2, 1, 3, 5, 4):
        for g in range(GROUPS):
            gather_copy(g, number).start()

    def pass_on(g):
        for number in range(3):
            gather_copy(g, number).wait_recv()
        for number in (6, 8, 7):
            gather_copy(g, number).start()

    for load in loads[1:]:
        load.wait()
    small_loads[0].wait()
    lanes = iota((CY, CX), 1)
    group_of, place = lanes >> 4, lanes & 15

    def pack_level(k, carry):
        for m in range(3):
            value = roll_lanes(state[k, m * 8], 8)
            for i in range(1, 8):
                value = jnp.where(group_of == i, roll_lanes(state[k, m * 8 + i], 16 * i + 8), value)
            packed[k * 3 + m] = value
        return carry

    lax.fori_loop(0, LEV, pack_level, 0)
    planes = [(c, k) for c in range(2) for k in range(LEV)]
    spare = [jnp.where(lanes < 16, roll_lanes(courant_ref[c, k], 8), 0.0) for c, k in planes]
    for shift in (16, 32, 64):
        spare = [value + roll_lanes(value, shift) for value in spare]
    for e, value in enumerate(spare):
        packed[24 + e] = value
    quad = (lanes >> 2) & 3
    for n in range(10):
        for side, base in ((0, 4), (1, 8)):
            value = roll_lanes(packed[4 * n], -base)
            for t in range(1, 4):
                value = jnp.where(quad == t, roll_lanes(packed[4 * n + t], 4 * t - base), value)
            halo_out[side, n] = value
    halos = [
        remote(halo_out.at[side], halo_in.at[side], halo_send.at[side], halo_recv.at[side], (comp, target))
        for side, target in ((0, right), (1, left))
    ]
    for copy in halos:
        copy.start()

    def level_coefs(k, carry):
        for n, value in enumerate(stencil_coefs(courant_ref[0, k], courant_ref[1, k])):
            coef[k, n] = value
        return carry

    for k in range(LEV):
        level_coefs(k, 0)

    def transport_step(n, carry):
        k = n >> 2
        coefs = [coef[k, i] for i in range(5)]
        for f in range(FIELDS):
            state[k, f] = one_step(state[k, f], coefs)
        return carry

    def transport_level(k):
        coefs = [coef[k, i] for i in range(5)]
        for step in range(4):
            for f in range(FIELDS):
                state[k, f] = one_step(state[k, f], coefs)

    for g in range(GROUPS):
        pass_on(g)

    for copy in halos:
        copy.wait_recv()
    mid = (place >= 8) & (place < 12)

    def strip(side, p):
        n, t = p >> 2, p & 3
        if side == 0:
            return jnp.where(place < 4, roll_lanes(halo_in[0, n], -4 * t), roll_lanes(packed[p], -4))
        return jnp.where(mid, roll_lanes(halo_in[1, n], 8 - 4 * t), packed[p])

    for p in range(3 * LEV):
        for side in range(2):
            strips[side, p // 12, p % 12] = strip(side, p)
    for k in range(LEV):
        for side in range(2):
            values = stencil_coefs(strip(side, 24 + k), strip(side, 32 + k))
            for n, value in enumerate(values):
                strip_coef[side, k >> 2, k & 3, n] = value

    for number in (9, 11, 10):
        for g in range(GROUPS):
            gather_copy(g, number).start()

    def strip_step(n, carry):
        half = n >> 2
        for j in range(4):
            for side in range(2):
                coefs = [strip_coef[side, half, j, i] for i in range(5)]
                for m in range(3):
                    p = j * 3 + m
                    strips[side, half, p] = one_step(strips[side, half, p], coefs)
        return carry

    lax.fori_loop(0, 8, strip_step, 0)
    for p in range(3 * LEV):
        i, r = p // 12, p % 12
        packed[p] = jnp.where(place < 4, roll_lanes(strips[1, i, r], -4), strips[0, i, r])

    small_loads[3].wait()
    rows_p, rows_q = iota((WTAB * CY, CX), 0), iota((256, CX), 0)
    lane_p = iota((1, CX), 1) >> 3

    def scatter_copy(part, g, d):
        target = (1 - comp, tile if d == 0 else shifted((g + 2) % 3, d))
        return remote(
            outgoing.at[part, g, d],
            arrived.at[part, g, (4 - d) % 4],
            sc_send.at[part, g, d],
            sc_recv.at[part, g, d],
            target,
        )

    def remap(part, g, carry):
        for number in range(3, 9) if part == 0 else range(9, 12):
            gather_copy(g, number).wait_recv()
        if part == 0:
            table = jnp.zeros((CY, CX), F32)
            for p in range(16):
                rv, ru = p // 4, p % 4
                offset = ((-ru % 4) * 4 + (-rv % 4)) * 8
                moved = roll_lanes(gath[g, rv, ru, 0].astype(F32), p * 8 - offset)
                table = jnp.where((lanes >> 3) == p, moved, table)
            codes = table.astype(I32)
            for d in range(4):
                w_e, r_e, y_e = codes[d : d + 1], codes[4 + d : 5 + d], codes[8 + d : 9 + d]
                into = (rows_p == jnp.where(y_e > 0, w_e * CY + y_e - 1, -1)).astype(F32).astype(BF16)
                outof = (rows_q == lane_p * CY + r_e).astype(F32).astype(BF16)
                pick[g, d] = lax.dot_general(into, outof, NT, preferred_element_type=F32).astype(BF16)
        first = 1 + part * HALF
        for d in range(4):
            for pair in range(HALF // 2):
                blocks = jnp.concatenate(
                    [gath[g, :, :, first + 2 * pair + i].reshape(256, CX) for i in range(2)], axis=1
                )
                summed = jnp.dot(pick[g, d], blocks, preferred_element_type=F32).astype(BF16)
                for i in range(2):
                    for w in range(WTAB):
                        row = (d * HALF + 2 * pair + i) * CY
                        spread[w, row : row + CY] = summed[w * CY : (w + 1) * CY, i * CX : (i + 1) * CX]
        transport_level(3 * part + g)
        table_all = jnp.concatenate([weight[w] for w in range(WTAB)], axis=1)
        rows = HALF * CY
        for d in range(0, 4, 2):
            chosen = jnp.concatenate([spread[w, d * rows : (d + 2) * rows] for w in range(WTAB)], axis=1)
            result = lax.dot_general(chosen, table_all, NT, preferred_element_type=F32).astype(BF16)
            for i in range(2):
                outgoing[part, g, d + i] = result[i * rows : (i + 1) * rows].reshape(HALF, CY, CX)
        for d in range(4):
            scatter_copy(part, g, d).start()
        return carry

    for part in range(2):
        lax.fori_loop(0, GROUPS, lambda g, carry, part=part: remap(part, g, carry), 0)
    lax.fori_loop(24, 32, transport_step, 0)

    small_loads[1].wait()
    small_loads[2].wait()
    ratio = jnp.zeros((CY, CX), F32)
    gain = None
    gains, ratios = [], []
    for k in range(LEV):
        above = diff_ref[k] if k < LEV - 1 else jnp.zeros((CY, CX), F32)
        below = diff_ref[k - 1] if k > 0 else jnp.zeros((CY, CX), F32)
        inverse = 1.0 / (1.0 + below + above - below * ratio)
        ratio = above * inverse
        solve_coef[0, k] = inverse
        solve_coef[1, k] = below * inverse
        solve_coef[2, k] = ratio
        gain = inverse if k == 0 else below * inverse * gain
        gains.append(gain)
        ratios.append(ratio)
    value = jnp.zeros((CY, CX), F32)
    for k in reversed(range(LEV)):
        value = gains[k] + ratios[k] * value
        gain_ref[k] = value * rate_ref[...]

    edge = (lanes < 4) | (lanes >= CX - 4)

    def solve_fields(n, carry):
        m = n >> 1
        for j in range(4):
            f = n * 4 + j
            turn = CX - 4 - 16 * ((n & 1) * 4 + j)
            solved = jnp.zeros((CY, CX), F32)
            kept = []
            for k in range(LEV):
                value = jnp.where(edge, pltpu.roll(packed[k * 3 + m], turn, 1), state[k, f])
                solved = solve_coef[0, k] * value + solve_coef[1, k] * solved
                kept.append(solved)
            upper = kept[-1]
            state[LEV - 1, f] = upper
            for k in reversed(range(LEV - 1)):
                upper = kept[k] + solve_coef[2, k] * upper
                state[k, f] = upper
        return carry

    lax.fori_loop(0, FIELDS // 4, solve_fields, 0)

    for part in range(2):
        for g in range(GROUPS):
            for d in range(4):
                scatter_copy(part, g, d).wait_recv()
            total = arrived[part, g, 0].astype(F32)
            for d in range(1, 4):
                total = total + arrived[part, g, d].astype(F32)
            start = (2 * g + part) * HALF
            incoming_ref[start : start + HALF] = total

    def finish(g, carry):
        for number in range(12):
            gather_copy(g, number).wait_send()
        for part in range(2):
            for d in range(4):
                scatter_copy(part, g, d).wait_send()
        return carry

    lax.fori_loop(0, GROUPS, finish, 0)
    for copy in halos:
        copy.wait_send()


def per_device(
    state_field,
    courant,
    diffusivity,
    coupling_rate,
    weight_table,
    source_row,
    destination_tile_ids,
    dest_row,
    weight_slot,
):
    vmem, hbm = pl.BlockSpec(memory_space=pltpu.VMEM), pl.BlockSpec(memory_space=pltpu.HBM)
    plane = (CY, CX)
    solved, gain, incoming = pl.pallas_call(
        kernel,
        out_shape=(
            pltpu.VMEM((LEV, FIELDS) + plane, F32),
            pltpu.VMEM((LEV,) + plane, F32),
            pltpu.VMEM((FIELDS,) + plane, F32),
        ),
        in_specs=[hbm] * 9,
        out_specs=(vmem, vmem, vmem),
        scratch_shapes=[
            pltpu.VMEM((2, LEV) + plane, F32),
            pltpu.VMEM((LEV,) + plane, F32),
            pltpu.VMEM(plane, F32),
            pltpu.VMEM((4, ENTRIES), I32),
            pltpu.VMEM((WTAB, CX, CX), BF16),
            pltpu.VMEM((40,) + plane, F32),
            pltpu.VMEM((2, 2, 12) + plane, F32),
            pltpu.VMEM((2, 2, 4, 5) + plane, F32),
            pltpu.VMEM((2, 10) + plane, F32),
            pltpu.VMEM((2, 10) + plane, F32),
            pltpu.VMEM((LEV, 5) + plane, F32),
            pltpu.VMEM((GROUPS, 4, 4, SLABS) + plane, BF16),
            pltpu.VMEM((GROUPS, 4, WTAB * CY, 256), BF16),
            pltpu.VMEM((WTAB, 4 * HALF * CY, CX), BF16),
            pltpu.VMEM((2, GROUPS, 4, HALF) + plane, BF16),
            pltpu.VMEM((2, GROUPS, 4, HALF) + plane, BF16),
            pltpu.VMEM((3, LEV) + plane, F32),
            pltpu.SemaphoreType.DMA((LEV,)),
            pltpu.SemaphoreType.DMA((4,)),
            pltpu.SemaphoreType.DMA((4,)),
            pltpu.SemaphoreType.DMA((GROUPS, 12)),
            pltpu.SemaphoreType.DMA((GROUPS, 12)),
            pltpu.SemaphoreType.DMA((2,)),
            pltpu.SemaphoreType.DMA((2,)),
            pltpu.SemaphoreType.DMA((2, GROUPS, 4)),
            pltpu.SemaphoreType.DMA((2, GROUPS, 4)),
        ],
        compiler_params=pltpu.CompilerParams(
            collective_id=0, has_side_effects=True, vmem_limit_bytes=60 * 2**20
        ),
        name="interval",
    )(
        state_field[0],
        courant[0],
        diffusivity[0],
        coupling_rate[0],
        weight_table,
        source_row[0],
        destination_tile_ids.reshape(1, ENTRIES),
        dest_row[0],
        weight_slot[0],
    )
    return (solved + gain[:, None] * incoming[None])[None]


def solution(mesh):
    return jax.shard_map(
        per_device,
        mesh=mesh,
        in_specs=(
            P("comp", None, None, None, "tile"),
            P("comp", None, None, None, "tile"),
            P("comp", None, None, "tile"),
            P("comp", None, "tile"),
            P(),
            P("comp", "tile", None),
            P("comp", "tile", None, None),
            P("comp", "tile", None),
            P("comp", "tile", None),
        ),
        out_specs=P("comp", None, None, None, "tile"),
        check_vma=False,
    )
```

```python
import jax
import jax.numpy as jnp
from jax import lax
from jax.experimental import pallas as pl
from jax.experimental.pallas import tpu as pltpu
from jax.sharding import PartitionSpec as P

MESH = pl.DeviceIdType.MESH
NT = (((1,), (1,)), ((), ()))
LEV, FIELDS, CY, CX = 8, 24, 16, 128
ENTRIES, WTAB = 384, 32
GROUPS = 3
GF = FIELDS // GROUPS
HALF = GF // 2
SLABS = GF + 1
CUT = HALF + 1
AXES = ((0, 1, 2), (1, 2, 0), (2, 0, 1))
F32, BF16, I32 = jnp.float32, jnp.bfloat16, jnp.int32


def iota(shape, dim):
    return lax.broadcasted_iota(I32, shape, dim)


def roll_lanes(value, shift):
    return pltpu.roll(value, shift % CX, 1)


def stencil_coefs(cx, cy):
    rows = iota(cx.shape, 0)
    cxp, cxm = jnp.maximum(cx, 0.0), jnp.minimum(cx, 0.0)
    cy = jnp.where(rows < CY - 1, cy, 0.0)
    cyp, cym = jnp.maximum(cy, 0.0), jnp.minimum(cy, 0.0)
    west = roll_lanes(cxp, 1)
    south = pltpu.roll(cyp, 1, 0)
    centre = 1.0 - cxp + roll_lanes(cxm, 1) - cyp + pltpu.roll(cym, 1, 0)
    return centre, -cxm, west, -cym, south


def one_step(a, coefs):
    centre, east, west, north, south = coefs
    return (
        centre * a
        + east * roll_lanes(a, CX - 1)
        + west * roll_lanes(a, 1)
        + north * pltpu.roll(a, CY - 1, 0)
        + south * pltpu.roll(a, 1, 0)
    )


def kernel(
    state_hbm,
    courant_hbm,
    diff_hbm,
    rate_hbm,
    weight_hbm,
    srow_hbm,
    dest_hbm,
    drow_hbm,
    wslot_hbm,
    state,
    gain_ref,
    incoming_ref,
    courant_ref,
    diff_ref,
    rate_ref,
    entries,
    weight,
    packed,
    strips,
    strip_coef,
    halo_out,
    halo_in,
    coef,
    gath,
    pick,
    spread,
    outgoing,
    arrived,
    solve_coef,
    load_sem,
    entry_sem,
    small_sem,
    ag_send,
    ag_recv,
    halo_send,
    halo_recv,
    sc_send,
    sc_recv,
):
    comp, tile = lax.axis_index("comp"), lax.axis_index("tile")
    coords = (tile >> 4, (tile >> 2) & 3, tile & 3)

    def shifted(axis, step):
        place = 4 - 2 * axis
        here = (tile >> place) & 3
        return tile + ((((here + step) & 3) - here) << place)

    right, left = (tile + 1) & 63, (tile + 63) & 63
    barrier = pltpu.get_barrier_semaphore()
    greeted = [(comp, shifted(axis, step)) for axis in range(3) for step in (1, 2, 3)]
    greeted += [(comp, right), (comp, left), (1 - comp, tile)]
    greeted += [(1 - comp, shifted(axis, step)) for axis in range(3) for step in (1, 2, 3)]
    for target in greeted:
        pl.semaphore_signal(barrier, inc=1, device_id=target, device_id_type=MESH)

    loads = [
        pltpu.make_async_copy(state_hbm.at[k], state.at[k], load_sem.at[k]) for k in range(LEV)
    ]
    entry_loads = [
        pltpu.make_async_copy(source, entries.at[pl.ds(n, 1)], entry_sem.at[n])
        for n, source in enumerate((dest_hbm, srow_hbm, drow_hbm, wslot_hbm))
    ]
    small_loads = [
        pltpu.make_async_copy(source, target, small_sem.at[n])
        for n, (source, target) in enumerate(
            ((courant_hbm, courant_ref), (diff_hbm, diff_ref), (rate_hbm, rate_ref), (weight_hbm, weight))
        )
    ]
    loads[0].start()
    for load in entry_loads:
        load.start()
    small_loads[0].start()
    for load in loads[1:]:
        load.start()
    for load in small_loads[1:]:
        load.start()

    for load in entry_loads:
        load.wait()
    targets, srow, drow, wslot = (entries[n : n + 1] for n in range(4))
    named = (iota((64, ENTRIES), 0) == targets).astype(F32)
    before = (iota((ENTRIES, ENTRIES), 0) < iota((ENTRIES, ENTRIES), 1)).astype(F32)
    counts = jnp.dot(named.astype(BF16), before.astype(BF16), preferred_element_type=F32)
    rank = jnp.sum(named * counts, axis=0, keepdims=True).astype(I32)
    rel = (
        ((targets >> 4) - coords[0]) & 3,
        ((targets >> 2) - coords[1]) & 3,
        (targets - coords[2]) & 3,
    )
    kind, quarter = iota((16, ENTRIES), 0) >> 2, iota((16, ENTRIES), 0) & 3
    values = jnp.where(kind == 0, wslot, jnp.where(kind == 1, srow, drow + 1))
    for g, (u, v, q) in enumerate(AXES):
        spot = (rel[u] * 4 + rel[v]) * 8 + rank
        hot = (iota((CX, ENTRIES), 0) == spot).astype(F32).astype(BF16)
        kept = jnp.where((quarter == rel[q]) & (kind < 3), values, 0)
        table = lax.dot_general(kept.astype(F32).astype(BF16), hot, NT, preferred_element_type=F32)
        gath[g, 0, 0, 0] = table.astype(BF16)

    loads[0].wait()
    for g in range(GROUPS):
        gath[g, 0, 0, 1:] = state[0, g * GF : (g + 1) * GF].astype(BF16)

    pl.semaphore_wait(barrier, len(greeted))

    def remote(src, dst, send, recv, target):
        return pltpu.make_async_remote_copy(
            src_ref=src,
            dst_ref=dst,
            send_sem=send,
            recv_sem=recv,
            device_id=target,
            device_id_type=MESH,
        )

    parts = (pl.ds(0, CUT), pl.ds(CUT, SLABS - CUT))

    def gather_copy(g, number):
        u, v = g, (g + 1) % 3
        step = number % 3 + 1
        there = 4 - step
        others = pl.ds(1, 3)
        src, dst, axis = (
            (gath.at[g, 0, 0], gath.at[g, 0, there], u),
            (gath.at[g, 0, 0, parts[0]], gath.at[g, there, 0, parts[0]], v),
            (gath.at[g, 0, others, parts[0]], gath.at[g, there, others, parts[0]], v),
            (gath.at[g, 0, :, parts[1]], gath.at[g, there, :, parts[1]], v),
        )[number // 3]
        return remote(
            src, dst, ag_send.at[g, number], ag_recv.at[g, number], (comp, shifted(axis, step))
        )

    for number in (0, 2, 1, 3, 5, 4):
        for g in range(GROUPS):
            gather_copy(g, number).start()

    def pass_on(g):
        for number in range(3):
            gather_copy(g, number).wait_recv()
        for number in (6, 8, 7):
            gather_copy(g, number).start()

    for load in loads[1:]:
        load.wait()
    small_loads[0].wait()
    lanes = iota((CY, CX), 1)
    group_of, place = lanes >> 4, lanes & 15

    def pack_level(k, carry):
        for m in range(3):
            value = roll_lanes(state[k, m * 8], 8)
            for i in range(1, 8):
                value = jnp.where(group_of == i, roll_lanes(state[k, m * 8 + i], 16 * i + 8), value)
            packed[k * 3 + m] = value
        return carry

    lax.fori_loop(0, LEV, pack_level, 0)
    planes = [(c, k) for c in range(2) for k in range(LEV)]
    spare = [jnp.where(lanes < 16, roll_lanes(courant_ref[c, k], 8), 0.0) for c, k in planes]
    for shift in (16, 32, 64):
        spare = [value + roll_lanes(value, shift) for value in spare]
    for e, value in enumerate(spare):
        packed[24 + e] = value
    quad = (lanes >> 2) & 3
    for n in range(10):
        for side, base in ((0, 4), (1, 8)):
            value = roll_lanes(packed[4 * n], -base)
            for t in range(1, 4):
                value = jnp.where(quad == t, roll_lanes(packed[4 * n + t], 4 * t - base), value)
            halo_out[side, n] = value
    halos = [
        remote(halo_out.at[side], halo_in.at[side], halo_send.at[side], halo_recv.at[side], (comp, target))
        for side, target in ((0, right), (1, left))
    ]
    for copy in halos:
        copy.start()

    def level_coefs(k, carry):
        for n, value in enumerate(stencil_coefs(courant_ref[0, k], courant_ref[1, k])):
            coef[k, n] = value
        return carry

    for k in range(LEV):
        level_coefs(k, 0)

    def transport_step(n, carry):
        k = n >> 2
        coefs = [coef[k, i] for i in range(5)]
        for f in range(FIELDS):
            state[k, f] = one_step(state[k, f], coefs)
        return carry

    def transport_level(k):
        coefs = [coef[k, i] for i in range(5)]
        for step in range(4):
            for f in range(FIELDS):
                state[k, f] = one_step(state[k, f], coefs)

    for g in range(GROUPS):
        pass_on(g)

    for copy in halos:
        copy.wait_recv()
    mid = (place >= 8) & (place < 12)

    def strip(side, p):
        n, t = p >> 2, p & 3
        if side == 0:
            return jnp.where(place < 4, roll_lanes(halo_in[0, n], -4 * t), roll_lanes(packed[p], -4))
        return jnp.where(mid, roll_lanes(halo_in[1, n], 8 - 4 * t), packed[p])

    for p in range(3 * LEV):
        for side in range(2):
            strips[side, p // 12, p % 12] = strip(side, p)
    for k in range(LEV):
        for side in range(2):
            values = stencil_coefs(strip(side, 24 + k), strip(side, 32 + k))
            for n, value in enumerate(values):
                strip_coef[side, k >> 2, k & 3, n] = value

    for number in (9, 11, 10):
        for g in range(GROUPS):
            gather_copy(g, number).start()

    def strip_step(n, carry):
        half = n >> 2
        for j in range(4):
            for side in range(2):
                coefs = [strip_coef[side, half, j, i] for i in range(5)]
                for m in range(3):
                    p = j * 3 + m
                    strips[side, half, p] = one_step(strips[side, half, p], coefs)
        return carry

    lax.fori_loop(0, 8, strip_step, 0)
    for p in range(3 * LEV):
        i, r = p // 12, p % 12
        packed[p] = jnp.where(place < 4, roll_lanes(strips[1, i, r], -4), strips[0, i, r])

    small_loads[1].wait()
    small_loads[2].wait()
    ratio = jnp.zeros((CY, CX), F32)
    gain = None
    gains, ratios = [], []
    for k in range(LEV):
        above = diff_ref[k] if k < LEV - 1 else jnp.zeros((CY, CX), F32)
        below = diff_ref[k - 1] if k > 0 else jnp.zeros((CY, CX), F32)
        inverse = 1.0 / (1.0 + below + above - below * ratio)
        ratio = above * inverse
        solve_coef[0, k] = inverse
        solve_coef[1, k] = below * inverse
        solve_coef[2, k] = ratio
        gain = inverse if k == 0 else below * inverse * gain
        gains.append(gain)
        ratios.append(ratio)
    value = jnp.zeros((CY, CX), F32)
    for k in reversed(range(LEV)):
        value = gains[k] + ratios[k] * value
        gain_ref[k] = value * rate_ref[...]

    small_loads[3].wait()
    rows_p, rows_q = iota((WTAB * CY, CX), 0), iota((256, CX), 0)
    lane_p = iota((1, CX), 1) >> 3

    def scatter_copy(part, g, d):
        target = (1 - comp, tile if d == 0 else shifted((g + 2) % 3, d))
        return remote(
            outgoing.at[part, g, d],
            arrived.at[part, g, (4 - d) % 4],
            sc_send.at[part, g, d],
            sc_recv.at[part, g, d],
            target,
        )

    def remap(part, g, carry):
        for number in range(3, 9) if part == 0 else range(9, 12):
            gather_copy(g, number).wait_recv()
        if part == 0:
            table = jnp.zeros((CY, CX), F32)
            for p in range(16):
                rv, ru = p // 4, p % 4
                offset = ((-ru % 4) * 4 + (-rv % 4)) * 8
                moved = roll_lanes(gath[g, rv, ru, 0].astype(F32), p * 8 - offset)
                table = jnp.where((lanes >> 3) == p, moved, table)
            codes = table.astype(I32)
            for d in range(4):
                w_e, r_e, y_e = codes[d : d + 1], codes[4 + d : 5 + d], codes[8 + d : 9 + d]
                into = (rows_p == jnp.where(y_e > 0, w_e * CY + y_e - 1, -1)).astype(F32).astype(BF16)
                outof = (rows_q == lane_p * CY + r_e).astype(F32).astype(BF16)
                pick[g, d] = lax.dot_general(into, outof, NT, preferred_element_type=F32).astype(BF16)
        first = 1 + part * HALF
        for d in range(4):
            for pair in range(HALF // 2):
                blocks = jnp.concatenate(
                    [gath[g, :, :, first + 2 * pair + i].reshape(256, CX) for i in range(2)], axis=1
                )
                summed = jnp.dot(pick[g, d], blocks, preferred_element_type=F32).astype(BF16)
                for i in range(2):
                    for w in range(WTAB):
                        row = (d * HALF + 2 * pair + i) * CY
                        spread[w, row : row + CY] = summed[w * CY : (w + 1) * CY, i * CX : (i + 1) * CX]
        transport_level(3 * part + g)
        table_all = jnp.concatenate([weight[w] for w in range(WTAB)], axis=1)
        rows = HALF * CY
        for d in range(0, 4, 2):
            chosen = jnp.concatenate([spread[w, d * rows : (d + 2) * rows] for w in range(WTAB)], axis=1)
            result = lax.dot_general(chosen, table_all, NT, preferred_element_type=F32).astype(BF16)
            for i in range(2):
                outgoing[part, g, d + i] = result[i * rows : (i + 1) * rows].reshape(HALF, CY, CX)
        for d in (2, 1, 3, 0):
            scatter_copy(part, g, d).start()
        return carry

    for part in range(2):
        lax.fori_loop(0, GROUPS, lambda g, carry, part=part: remap(part, g, carry), 0)
    lax.fori_loop(24, 32, transport_step, 0)

    edge = (lanes < 4) | (lanes >= CX - 4)

    def solve_fields(n, carry):
        m = n >> 1
        for j in range(4):
            f = n * 4 + j
            turn = CX - 4 - 16 * ((n & 1) * 4 + j)
            solved = jnp.zeros((CY, CX), F32)
            kept = []
            for k in range(LEV):
                value = jnp.where(edge, pltpu.roll(packed[k * 3 + m], turn, 1), state[k, f])
                solved = solve_coef[0, k] * value + solve_coef[1, k] * solved
                kept.append(solved)
            upper = kept[-1]
            state[LEV - 1, f] = upper
            for k in reversed(range(LEV - 1)):
                upper = kept[k] + solve_coef[2, k] * upper
                state[k, f] = upper
        return carry

    lax.fori_loop(0, FIELDS // 4, solve_fields, 0)

    for part in range(2):
        for g in range(GROUPS):
            for d in range(4):
                scatter_copy(part, g, d).wait_recv()
            total = arrived[part, g, 0].astype(F32)
            for d in range(1, 4):
                total = total + arrived[part, g, d].astype(F32)
            start = (2 * g + part) * HALF
            incoming_ref[start : start + HALF] = total

    def finish(g, carry):
        for number in range(12):
            gather_copy(g, number).wait_send()
        for part in range(2):
            for d in range(4):
                scatter_copy(part, g, d).wait_send()
        return carry

    lax.fori_loop(0, GROUPS, finish, 0)
    for copy in halos:
        copy.wait_send()


def per_device(
    state_field,
    courant,
    diffusivity,
    coupling_rate,
    weight_table,
    source_row,
    destination_tile_ids,
    dest_row,
    weight_slot,
):
    vmem, hbm = pl.BlockSpec(memory_space=pltpu.VMEM), pl.BlockSpec(memory_space=pltpu.HBM)
    plane = (CY, CX)
    solved, gain, incoming = pl.pallas_call(
        kernel,
        out_shape=(
            pltpu.VMEM((LEV, FIELDS) + plane, F32),
            pltpu.VMEM((LEV,) + plane, F32),
            pltpu.VMEM((FIELDS,) + plane, F32),
        ),
        in_specs=[hbm] * 9,
        out_specs=(vmem, vmem, vmem),
        scratch_shapes=[
            pltpu.VMEM((2, LEV) + plane, F32),
            pltpu.VMEM((LEV,) + plane, F32),
            pltpu.VMEM(plane, F32),
            pltpu.VMEM((4, ENTRIES), I32),
            pltpu.VMEM((WTAB, CX, CX), BF16),
            pltpu.VMEM((40,) + plane, F32),
            pltpu.VMEM((2, 2, 12) + plane, F32),
            pltpu.VMEM((2, 2, 4, 5) + plane, F32),
            pltpu.VMEM((2, 10) + plane, F32),
            pltpu.VMEM((2, 10) + plane, F32),
            pltpu.VMEM((LEV, 5) + plane, F32),
            pltpu.VMEM((GROUPS, 4, 4, SLABS) + plane, BF16),
            pltpu.VMEM((GROUPS, 4, WTAB * CY, 256), BF16),
            pltpu.VMEM((WTAB, 4 * HALF * CY, CX), BF16),
            pltpu.VMEM((2, GROUPS, 4, HALF) + plane, BF16),
            pltpu.VMEM((2, GROUPS, 4, HALF) + plane, BF16),
            pltpu.VMEM((3, LEV) + plane, F32),
            pltpu.SemaphoreType.DMA((LEV,)),
            pltpu.SemaphoreType.DMA((4,)),
            pltpu.SemaphoreType.DMA((4,)),
            pltpu.SemaphoreType.DMA((GROUPS, 12)),
            pltpu.SemaphoreType.DMA((GROUPS, 12)),
            pltpu.SemaphoreType.DMA((2,)),
            pltpu.SemaphoreType.DMA((2,)),
            pltpu.SemaphoreType.DMA((2, GROUPS, 4)),
            pltpu.SemaphoreType.DMA((2, GROUPS, 4)),
        ],
        compiler_params=pltpu.CompilerParams(
            collective_id=0, has_side_effects=True, vmem_limit_bytes=60 * 2**20
        ),
        name="interval",
    )(
        state_field[0],
        courant[0],
        diffusivity[0],
        coupling_rate[0],
        weight_table,
        source_row[0],
        destination_tile_ids.reshape(1, ENTRIES),
        dest_row[0],
        weight_slot[0],
    )
    return (solved + gain[:, None] * incoming[None])[None]


def solution(mesh):
    return jax.shard_map(
        per_device,
        mesh=mesh,
        in_specs=(
            P("comp", None, None, None, "tile"),
            P("comp", None, None, None, "tile"),
            P("comp", None, None, "tile"),
            P("comp", None, "tile"),
            P(),
            P("comp", "tile", None),
            P("comp", "tile", None, None),
            P("comp", "tile", None),
            P("comp", "tile", None),
        ),
        out_specs=P("comp", None, None, None, "tile"),
        check_vma=False,
    )
```
